32 devices in a mesh: ctx: 8 (over z, x), ch: 4 (over y, core).
Axes of the slice: x: 2, y: 2, z: 4, core: 2. Of those that a mesh axis runs over, the one named last changes fastest.
Arguments:
- streams: bfloat16 [3, 8192, 2048], P(None, ('ch', 'ctx')), may hold values from -6 to 6
- short_taps: float32 [3, 512, 7], P(None, 'ch'), may hold values from -3 to 3
- pole_rates: float32 [512, 16], P('ch'), may hold values from 2.4414063e-05 to 0.2, as said below
- residues: float32 [512, 16], P('ch'), may hold values from -0.6 to 0.6
- skip: float32 [8192], P('ch'), may hold values from -1 to 1
- gain: float32 [8192], P('ch'), may hold values from 0.1 to 1.9
Outputs:
- normed: bfloat16 [8192, 2048], P('ch', 'ctx')
The draws below stay inside these ranges and needn't reach their ends.
Inputs may be any that keep to these rules, and one draw needn't show every extreme that they name: `pole_rates`: decay rates, all positive.
All inputs are finite; a program needn't handle non-finite values.
Results may differ from the reference program's by a relative error of at most 0.001.
Values may be sent and summed in bfloat16 or wider, within the bound.
A program may use at most 128 MiB of HBM per device.

```python
import math
import jax
import jax.numpy as jnp
from jax import lax

D = 8192
GROUPS = 512
POLES = 16
SHORT = 7
BLOCK = 128
SEQ = 2048


def pole_law(key):
    keys = jax.random.split(jax.random.fold_in(key, 7), 3)
    shape_here = (GROUPS, POLES)
    slow_rates = jnp.exp(jax.random.uniform(keys[0], shape_here, jnp.float32, math.log(0.05 / SEQ), math.log(1.5 / SEQ)))
    fast_rates = jnp.exp(jax.random.uniform(keys[1], shape_here, jnp.float32, math.log(0.02), math.log(0.2)))
    share = 0.5
    keep_slow = jax.random.uniform(keys[2], shape_here, jnp.float32) < share
    return jnp.where(keep_slow, slow_rates, fast_rates)


def draw_pole_rates(key, part):
    return pole_law(key)


def draw_residues(key, part):
    rates_drawn = pole_law(key)
    residue_key = jax.random.fold_in(key, 13)
    base_values = jnp.clip(jax.random.normal(residue_key, (GROUPS, POLES), jnp.float32), -4.0, 4.0)
    return base_values * jnp.sqrt(2.0 * rates_drawn + 2.0 / SEQ) * 0.2


def levels(own_key, extent, pieces, low, top_value):
    level = 1.0
    for axis_at, blocks in pieces:
        steps = jax.random.uniform(jax.random.fold_in(jax.random.fold_in(own_key, 6), axis_at), (blocks,), jnp.float32, low / len(pieces), top_value / len(pieces))
        level = level * jnp.repeat(jnp.exp(steps), extent[axis_at] // blocks).reshape((-1,) + (1,) * (len(extent) - 1 - axis_at))
    return level


def scatter_about(rng, dims, scale, limit, cuts=(), held_as=jnp.bfloat16):
    level = levels(rng, dims, cuts, -0.22, 0.18) if cuts else 1.0
    result = jax.random.normal(rng, dims, jnp.float32) * scale * level
    return jnp.minimum(jnp.maximum(result, -limit), limit).astype(held_as)


def setup_inputs(seed: int = 0) -> dict:
    streams_of = jax.random.split(jax.random.key(seed), 7)
    streams = scatter_about(streams_of[0], (3, D, SEQ), 1.0, 6.0, ((1, 32),))
    short_taps = scatter_about(streams_of[1], (3, GROUPS, SHORT), 0.4, 3.0, ((1, 4),), jnp.float32)
    pole_rates = draw_pole_rates(jax.random.fold_in(streams_of[6], 71), 0)
    residues = draw_residues(jax.random.fold_in(streams_of[6], 71), 0)
    skip = jnp.clip(jax.random.uniform(streams_of[4], (D,), jnp.float32, -1.0, 1.0) * levels(streams_of[4], (D,), ((0, 4),), -0.4, 0.0), -1.0, 1.0)
    gain = jnp.clip(1.0 + 0.18 * jax.random.normal(streams_of[5], (D,), jnp.float32), 0.1, 1.9)
    return {"streams": streams, "short_taps": short_taps, "pole_rates": pole_rates, "residues": residues, "skip": skip, "gain": gain}


HIGHEST_PRECISION = lax.Precision.HIGHEST

def short_filter(extended, short_taps, groups, length):
    reach_back = short_taps.shape[2] - 1
    channels = extended.shape[1]
    shaped = extended.reshape(3, groups, channels // groups, extended.shape[2])
    summed = jnp.zeros((3, groups, channels // groups, length), jnp.float32)
    for offset in range(short_taps.shape[2]):
        window = shaped[:, :, :, reach_back - offset:reach_back - offset + length].astype(jnp.float32)
        summed = summed + short_taps[:, :, offset][:, :, None, None] * window
    return summed

def kernel_table(pole_rates, residues, block):
    row_index = jnp.arange(block, dtype=jnp.int32)[:, None]
    col_index = jnp.arange(block, dtype=jnp.int32)[None, :]
    lag_flat = (row_index - col_index).reshape(-1)
    step_values = jnp.arange(block, dtype=jnp.int32).astype(jnp.float32)
    modal_row = jnp.einsum('gp,gpl->gl', residues, jnp.exp(-pole_rates[:, :, None] * step_values), precision=HIGHEST_PRECISION)
    picker = (jnp.arange(block, dtype=jnp.int32)[:, None] == lag_flat[None, :]).astype(jnp.float32)
    table = jnp.dot(modal_row, picker, precision=HIGHEST_PRECISION, preferred_element_type=jnp.float32)
    return table.reshape(modal_row.shape[0], block, block)

def compose(earlier, later_pair):
    return (earlier[0] * later_pair[0], later_pair[0] * earlier[1] + later_pair[1])

def block_terms(product, kernel, pole_rates, block):
    groups, group_width, length = product.shape
    block_count = length // block
    current = product.reshape(groups, group_width, block_count, block)
    inner_part = jnp.einsum('gsnk,gik->gsni', current, kernel, precision=HIGHEST_PRECISION)
    reverse_steps = (block - 1 - jnp.arange(block, dtype=jnp.int32)).astype(jnp.float32)
    backward = jnp.exp(-pole_rates[:, :, None] * reverse_steps)
    end_states = jnp.einsum('gsnk,gpk->gsnp', current, backward, precision=HIGHEST_PRECISION)
    decays = jnp.broadcast_to(jnp.exp(-pole_rates * block)[:, None, None, :], end_states.shape)
    lifted, prefix = lax.associative_scan(compose, (decays, end_states), axis=2)
    return (inner_part, prefix)

def finish_terms(inner_part, prefix, state_in, pole_rates, residues, block):
    groups, group_width, block_count, block_size = inner_part.shape
    counts = jnp.arange(1, block_count + 1, dtype=jnp.int32).astype(jnp.float32) * block
    powers = jnp.exp(-pole_rates[:, None, :] * counts[None, :, None])
    after_block = prefix + powers[:, None, :, :] * state_in[:, :, None, :]
    starts = jnp.concatenate([state_in[:, :, None, :], after_block[:, :, :-1, :]], axis=2)
    lift_steps = jnp.arange(1, block + 1, dtype=jnp.int32).astype(jnp.float32)
    lift_table = residues[:, :, None] * jnp.exp(-pole_rates[:, :, None] * lift_steps)
    carried = jnp.einsum('gsnp,gpi->gsni', starts, lift_table, precision=HIGHEST_PRECISION)
    return (inner_part + carried).reshape(groups, group_width, block_count * block)

def reference(streams, short_taps, pole_rates, residues, skip, gain):
    group_size = D // GROUPS
    length = streams.shape[2]

    def one_group(group_index):
        group_rows = lax.dynamic_slice_in_dim(streams, group_index * group_size, group_size, 1)
        taps_here = lax.dynamic_slice_in_dim(short_taps, group_index, 1, 1)
        rates_here = lax.dynamic_slice_in_dim(pole_rates, group_index, 1, 0)
        residue_here = lax.dynamic_slice_in_dim(residues, group_index, 1, 0)
        skip_here = lax.dynamic_slice_in_dim(skip, group_index * group_size, group_size, 0)
        extended = jnp.concatenate([jnp.zeros((3, group_size, SHORT - 1), streams.dtype), group_rows], axis=2)
        filtered = short_filter(extended, taps_here, 1, length)
        product = filtered[1] * filtered[2]
        kernel = kernel_table(rates_here, residue_here, BLOCK)
        inner_part, prefix = block_terms(product, kernel, rates_here, BLOCK)
        state_zero = jnp.zeros((1, group_size, POLES), jnp.float32)
        convolved = finish_terms(inner_part, prefix, state_zero, rates_here, residue_here, BLOCK)
        gated_value = filtered[0] * (convolved + skip_here[None, :, None] * product)
        return gated_value[0]
    gated_value = lax.map(one_group, jnp.arange(GROUPS, dtype=jnp.int32)).reshape(D, length)
    mean_square = lax.optimization_barrier(jnp.mean(gated_value * gated_value, axis=0))
    return (gated_value * gain[:, None] * lax.rsqrt(mean_square + 1e-05)[None, :]).astype(jnp.bfloat16)
```

```python
import functools

import jax
import jax.numpy as jnp
from jax import lax
from jax.experimental import pallas as pl
from jax.experimental.pallas import tpu as pltpu
from jax.sharding import PartitionSpec as P

BLOCK = 128


def split(value):
    high = value.astype(jnp.bfloat16)
    low = (value - high.astype(jnp.float32)).astype(jnp.bfloat16)
    return high, low


def halves(array):
    return array[:, :BLOCK] + array[:, BLOCK:]


def rolled(row):
    return pltpu.roll(
        jnp.broadcast_to(row, (BLOCK, BLOCK)), 0, 1, stride=1, stride_axis=0
    )


def mix(streams_ref, taps_ref, columns_ref, gated_ref, sums_ref, squares):
    step = pl.program_id(0)
    width, length = streams_ref.shape[1:]
    blocks = length // BLOCK
    per_device = gated_ref.shape[2] // BLOCK
    row_index = lax.broadcasted_iota(jnp.int32, (BLOCK, BLOCK), 0)
    col_index = lax.broadcasted_iota(jnp.int32, (BLOCK, BLOCK), 1)
    causal = col_index >= row_index

    filtered = []
    for m in range(3):
        table = rolled(taps_ref[0, m : m + 1, :])
        high_now, low_now = split(jnp.where(causal, table, 0.0))
        high_before, low_before = split(jnp.where(causal, 0.0, table))
        weights = jnp.concatenate(
            [
                jnp.concatenate([high_before, low_before], axis=1),
                jnp.concatenate([high_now, low_now], axis=1),
            ],
            axis=0,
        )
        pieces = [streams_ref[m, :, n * BLOCK : (n + 1) * BLOCK] for n in range(blocks)]
        now = jnp.concatenate(pieces, axis=0)
        before = jnp.concatenate([jnp.zeros_like(pieces[0])] + pieces[:-1], axis=0)
        both = jnp.concatenate([before, now], axis=1)
        filtered.append(halves(jnp.dot(both, weights, preferred_element_type=jnp.float32)))
    product = filtered[1] * filtered[2]
    product_high, product_low = split(product)
    pair = jnp.concatenate([product_high, product_low], axis=1)

    skip = columns_ref[:, 0:1]
    gain = columns_ref[:, 1:2]
    rates = columns_ref[:, 2:3]
    residues = columns_ref[:, 3:4]
    lags = lax.broadcasted_iota(jnp.int32, (width, BLOCK), 1).astype(jnp.float32)
    modes = residues * jnp.exp(-rates * lags)
    table_high, table_low = split(
        jnp.where(causal, rolled(jnp.sum(modes, axis=0, keepdims=True)), 0.0)
    )
    table_row = jnp.concatenate([table_high, table_low], axis=1)
    summed = jnp.dot(
        pair,
        jnp.concatenate([table_row, table_row], axis=0),
        preferred_element_type=jnp.float32,
    )

    back_high, back_low = split(jnp.exp(-rates * (BLOCK - 1 - lags)))
    back = jnp.concatenate(
        [
            jnp.concatenate([back_high, back_high], axis=1),
            jnp.concatenate([back_low, back_low], axis=1),
        ],
        axis=0,
    )
    ends = lax.dot_general(
        back, pair, (((1,), (1,)), ((), ())), preferred_element_type=jnp.float32
    )
    states = ends[:width] + ends[width:]
    lane = lax.broadcasted_iota(jnp.int32, states.shape, 1)
    reach = 1
    while reach < blocks:
        earlier = pltpu.roll(states, reach * width, 1)
        decay = jnp.exp(-rates * (BLOCK * reach))
        states = states + jnp.where(lane >= reach * width, decay * earlier, 0.0)
        reach *= 2
    starts = jnp.where(lane >= width, pltpu.roll(states, width, 1), 0.0)
    starts_high, starts_low = split(starts)
    starts = jnp.concatenate(
        [starts_high.astype(jnp.float32), starts_low.astype(jnp.float32)], axis=0
    ).T.astype(jnp.bfloat16)
    lift_high, lift_low = split(residues * jnp.exp(-rates * (lags + 1.0)))
    lift_row = jnp.concatenate([lift_high, lift_low], axis=1)
    summed = summed + jnp.dot(
        starts,
        jnp.concatenate([lift_row, lift_row], axis=0),
        preferred_element_type=jnp.float32,
    )

    shaped = (blocks, width, BLOCK)
    gated = filtered[0].reshape(shaped) * (
        halves(summed).reshape(shaped) + skip[None] * product.reshape(shaped)
    )
    squared = jnp.sum((gated * gated).reshape(blocks, width // 8, 8, BLOCK), axis=1)

    @pl.when(step == 0)
    def _():
        squares[...] = squared

    @pl.when(step > 0)
    def _():
        squares[...] += squared

    scaled = gated * gain[None]
    for n in range(blocks):
        at = (n % per_device) * BLOCK
        gated_ref[n // per_device, :, at : at + BLOCK] = scaled[n]

    @pl.when(step == pl.num_programs(0) - 1)
    def _():
        for n in range(blocks):
            at = (n % per_device) * BLOCK
            row = n // per_device
            sums_ref[row : row + 1, at : at + BLOCK] = jnp.sum(
                squares[n], axis=0, keepdims=True
            )


def shards(total_channels, streams, short_taps, pole_rates, residues, skip, gain):
    owners = lax.axis_size("ctx")
    me = lax.axis_index("ctx")
    channels, length = streams.shape[1:]
    groups = pole_rates.shape[0] // owners
    width = channels // groups
    assert pole_rates.shape[1] == width
    own = length // owners
    taps = lax.dynamic_slice_in_dim(short_taps, me * groups, groups, 1)
    taps = jnp.pad(taps.transpose(1, 0, 2), ((0, 0), (0, 0), (0, BLOCK - taps.shape[2])))
    columns = jnp.stack(
        [
            lax.dynamic_slice_in_dim(skip, me * channels, channels),
            lax.dynamic_slice_in_dim(gain, me * channels, channels),
            lax.dynamic_slice_in_dim(pole_rates, me * groups, groups).reshape(-1),
            lax.dynamic_slice_in_dim(residues, me * groups, groups).reshape(-1),
        ],
        axis=1,
    )
    gated, sums = pl.pallas_call(
        mix,
        grid=(groups,),
        in_specs=[
            pl.BlockSpec((3, width, length), lambda g: (0, g, 0)),
            pl.BlockSpec((1, 3, BLOCK), lambda g: (g, 0, 0)),
            pl.BlockSpec((width, 4), lambda g: (g, 0)),
        ],
        out_specs=[
            pl.BlockSpec((owners, width, own), lambda g: (0, g, 0)),
            pl.BlockSpec((owners, own), lambda g: (0, 0)),
        ],
        out_shape=[
            jax.ShapeDtypeStruct((owners, channels, own), jnp.float32),
            jax.ShapeDtypeStruct((owners, own), jnp.float32),
        ],
        scratch_shapes=[pltpu.VMEM((length // BLOCK, 8, BLOCK), jnp.float32)],
        compiler_params=pltpu.CompilerParams(vmem_limit_bytes=48 * 1024 * 1024),
    )(streams, taps, columns)
    mean_square = lax.psum(sums, ("ctx", "ch")) / total_channels
    scaled = (gated * lax.rsqrt(mean_square + 1e-05)[:, None, :]).astype(jnp.bfloat16)
    moved = lax.all_to_all(scaled, "ctx", split_axis=0, concat_axis=0, tiled=True)
    return moved.reshape(owners * channels, own)


def solution(mesh):
    placed = (
        P(None, ("ch", "ctx"), None),
        P(None, "ch", None),
        P("ch", None),
        P("ch", None),
        P("ch"),
        P("ch"),
    )

    def whole(streams, *others):
        return jax.shard_map(
            functools.partial(shards, streams.shape[1]),
            mesh=mesh,
            in_specs=placed,
            out_specs=P("ch", "ctx"),
            check_vma=False,
        )(streams, *others)

    return whole
```

```python
import functools

import jax
import jax.numpy as jnp
from jax import lax
from jax.experimental import pallas as pl
from jax.experimental.pallas import tpu as pltpu
from jax.sharding import PartitionSpec as P

BLOCK = 128
MESH = pl.DeviceIdType.MESH


def split(value):
    high = value.astype(jnp.bfloat16)
    low = (value - high.astype(jnp.float32)).astype(jnp.bfloat16)
    return high, low


def halves(array):
    return array[:, :BLOCK] + array[:, BLOCK:]


def rolled(row):
    return pltpu.roll(
        jnp.broadcast_to(row, (BLOCK, BLOCK)), 0, 1, stride=1, stride_axis=0
    )


def one_group(streams_ref, taps_ref, columns_ref, gated_ref, at_group, width):
    length = streams_ref.shape[2]
    blocks = length // BLOCK
    per_device = gated_ref.shape[2] // BLOCK
    rows = slice(at_group * width, (at_group + 1) * width)
    row_index = lax.broadcasted_iota(jnp.int32, (BLOCK, BLOCK), 0)
    col_index = lax.broadcasted_iota(jnp.int32, (BLOCK, BLOCK), 1)
    causal = col_index >= row_index

    filtered = []
    for m in range(3):
        table = rolled(taps_ref[at_group, m : m + 1, :])
        high_now, low_now = split(jnp.where(causal, table, 0.0))
        high_before, low_before = split(jnp.where(causal, 0.0, table))
        weights = jnp.concatenate(
            [
                jnp.concatenate([high_before, low_before], axis=1),
                jnp.concatenate([high_now, low_now], axis=1),
            ],
            axis=0,
        )
        pieces = [streams_ref[m, rows, n * BLOCK : (n + 1) * BLOCK] for n in range(blocks)]
        now = jnp.concatenate(pieces, axis=0)
        before = jnp.concatenate([jnp.zeros_like(pieces[0])] + pieces[:-1], axis=0)
        both = jnp.concatenate([before, now], axis=1)
        filtered.append(halves(jnp.dot(both, weights, preferred_element_type=jnp.float32)))
    product = filtered[1] * filtered[2]
    product_high, product_low = split(product)
    pair = jnp.concatenate([product_high, product_low], axis=1)

    skip = columns_ref[rows, 0:1]
    gain = columns_ref[rows, 1:2]
    rates = columns_ref[rows, 2:3]
    residues = columns_ref[rows, 3:4]
    lags = lax.broadcasted_iota(jnp.int32, (width, BLOCK), 1).astype(jnp.float32)
    modes = residues * jnp.exp(-rates * lags)
    table_high, table_low = split(
        jnp.where(causal, rolled(jnp.sum(modes, axis=0, keepdims=True)), 0.0)
    )
    table_row = jnp.concatenate([table_high, table_low], axis=1)
    summed = jnp.dot(
        pair,
        jnp.concatenate([table_row, table_row], axis=0),
        preferred_element_type=jnp.float32,
    )

    back_high, back_low = split(jnp.exp(-rates * (BLOCK - 1 - lags)))
    back = jnp.concatenate(
        [
            jnp.concatenate([back_high, back_high], axis=1),
            jnp.concatenate([back_low, back_low], axis=1),
        ],
        axis=0,
    )
    ends = lax.dot_general(
        back, pair, (((1,), (1,)), ((), ())), preferred_element_type=jnp.float32
    )
    states = ends[:width] + ends[width:]
    lane = lax.broadcasted_iota(jnp.int32, states.shape, 1)
    reach = 1
    while reach < blocks:
        earlier = pltpu.roll(states, reach * width, 1)
        decay = jnp.exp(-rates * (BLOCK * reach))
        states = states + jnp.where(lane >= reach * width, decay * earlier, 0.0)
        reach *= 2
    starts = jnp.where(lane >= width, pltpu.roll(states, width, 1), 0.0)
    starts_high, starts_low = split(starts)
    starts = jnp.concatenate(
        [starts_high.astype(jnp.float32), starts_low.astype(jnp.float32)], axis=0
    ).T.astype(jnp.bfloat16)
    lift_high, lift_low = split(residues * jnp.exp(-rates * (lags + 1.0)))
    lift_row = jnp.concatenate([lift_high, lift_low], axis=1)
    summed = summed + jnp.dot(
        starts,
        jnp.concatenate([lift_row, lift_row], axis=0),
        preferred_element_type=jnp.float32,
    )

    shaped = (blocks, width, BLOCK)
    gated = filtered[0].reshape(shaped) * (
        halves(summed).reshape(shaped) + skip[None] * product.reshape(shaped)
    )
    squared = jnp.sum((gated * gated).reshape(blocks, width // 8, 8, BLOCK), axis=1)

    scaled = gated * gain[None]
    for n in range(blocks):
        at = (n % per_device) * BLOCK
        gated_ref[n // per_device, rows, at : at + BLOCK] = scaled[n]

    return squared


def mix(at_once, streams_ref, taps_ref, columns_ref, gated_ref, sums_ref, squares):
    step = pl.program_id(0)
    width = streams_ref.shape[1] // at_once
    blocks = streams_ref.shape[2] // BLOCK
    per_device = gated_ref.shape[2] // BLOCK
    parts = [
        one_group(streams_ref, taps_ref, columns_ref, gated_ref, i, width) for i in range(at_once)
    ]
    squared = sum(parts[1:], parts[0])

    @pl.when(step == 0)
    def _():
        squares[...] = squared

    @pl.when(step > 0)
    def _():
        squares[...] += squared

    @pl.when(step == pl.num_programs(0) - 1)
    def _():
        for n in range(blocks):
            at = (n % per_device) * BLOCK
            row = n // per_device
            sums_ref[row : row + 1, at : at + BLOCK] = jnp.sum(
                squares[n], axis=0, keepdims=True
            )


def send(totals_of, sums_ref, gated_ref, out_ref, across, column, along, staged, scales, *sems):
    across_sent, across_got, along_sent, along_got, block_sent, block_got, kept = sems
    owners, channels, own = gated_ref.shape
    across_count = lax.axis_size("ch")
    me = lax.axis_index("ctx")
    my_ch = lax.axis_index("ch")

    def peer_ctx(by):
        return {"ctx": lax.rem(me + by, owners)}

    def peer_ch(by):
        return {"ch": lax.rem(my_ch + by, across_count)}

    barrier = pltpu.get_barrier_semaphore()

    @pl.loop(1, across_count)
    def _(by):
        pl.semaphore_signal(barrier, inc=1, device_id=peer_ch(by), device_id_type=MESH)

    @pl.loop(1, owners)
    def _(by):
        pl.semaphore_signal(barrier, inc=1, device_id=peer_ctx(by), device_id_type=MESH)

    pl.semaphore_wait(barrier, across_count + owners - 2)

    def across_copy(by):
        return pltpu.make_async_remote_copy(
            src_ref=sums_ref,
            dst_ref=across.at[by],
            send_sem=across_sent.at[by],
            recv_sem=across_got.at[by],
            device_id=peer_ch(by),
            device_id_type=MESH,
        )

    def along_copy(by):
        return pltpu.make_async_remote_copy(
            src_ref=column,
            dst_ref=along.at[by],
            send_sem=along_sent.at[by],
            recv_sem=along_got.at[by],
            device_id=peer_ctx(by),
            device_id_type=MESH,
        )

    def block_copy(by):
        return pltpu.make_async_remote_copy(
            src_ref=staged.at[by],
            dst_ref=out_ref.at[pl.ds(pl.multiple_of(me * channels, 16), channels), :],
            send_sem=block_sent.at[by],
            recv_sem=block_got.at[by],
            device_id=peer_ctx(by),
            device_id_type=MESH,
        )

    def block_arrival(by):
        source = lax.rem(me + owners - by, owners)
        return pltpu.make_async_remote_copy(
            src_ref=staged.at[by],
            dst_ref=out_ref.at[pl.ds(pl.multiple_of(source * channels, 16), channels), :],
            send_sem=block_sent.at[by],
            recv_sem=block_got.at[by],
            device_id=peer_ctx(by),
            device_id_type=MESH,
        )

    @pl.loop(1, across_count)
    def _(by):
        across_copy(by).start()

    column[...] = sums_ref[...]

    @pl.loop(1, across_count)
    def _(by):
        across_copy(by).wait()
        column[...] += across[by]

    @pl.loop(1, owners)
    def _(by):
        along_copy(by).start()

    scales[...] = column[...]

    @pl.loop(1, owners)
    def _(by):
        along_copy(by).wait()
        scales[...] += along[by]

    scales[...] = lax.rsqrt(scales[...] / totals_of + 1e-05)

    def fill(by):
        target = lax.rem(me + by, owners)
        row = scales[pl.ds(target, 1), :]
        staged[by] = (gated_ref[target] * row).astype(jnp.bfloat16)

    @pl.loop(1, owners)
    def _(by):
        fill(by)
        block_copy(by).start()

    fill(0)
    mine = pltpu.make_async_copy(
        staged.at[0],
        out_ref.at[pl.ds(pl.multiple_of(me * channels, 16), channels), :],
        kept,
    )
    mine.start()
    mine.wait()

    @pl.loop(1, owners)
    def _(by):
        block_copy(by).wait_send()
        block_arrival(by).wait_recv()


def shards(total_channels, streams, short_taps, pole_rates, residues, skip, gain):
    owners = lax.axis_size("ctx")
    me = lax.axis_index("ctx")
    channels, length = streams.shape[1:]
    groups = pole_rates.shape[0] // owners
    width = channels // groups
    assert pole_rates.shape[1] == width
    own = length // owners
    taps = lax.dynamic_slice_in_dim(short_taps, me * groups, groups, 1)
    taps = jnp.pad(taps.transpose(1, 0, 2), ((0, 0), (0, 0), (0, BLOCK - taps.shape[2])))
    columns = jnp.stack(
        [
            lax.dynamic_slice_in_dim(skip, me * channels, channels),
            lax.dynamic_slice_in_dim(gain, me * channels, channels),
            lax.dynamic_slice_in_dim(pole_rates, me * groups, groups).reshape(-1),
            lax.dynamic_slice_in_dim(residues, me * groups, groups).reshape(-1),
        ],
        axis=1,
    )
    at_once = 2 if groups % 2 == 0 else 1
    gated, sums = pl.pallas_call(
        functools.partial(mix, at_once),
        grid=(groups // at_once,),
        in_specs=[
            pl.BlockSpec((3, at_once * width, length), lambda g: (0, g, 0)),
            pl.BlockSpec((at_once, 3, BLOCK), lambda g: (g, 0, 0)),
            pl.BlockSpec((at_once * width, 4), lambda g: (g, 0)),
        ],
        out_specs=[
            pl.BlockSpec((owners, at_once * width, own), lambda g: (0, g, 0)),
            pl.BlockSpec((owners, own), lambda g: (0, 0)),
        ],
        out_shape=[
            jax.ShapeDtypeStruct((owners, channels, own), jnp.float32),
            jax.ShapeDtypeStruct((owners, own), jnp.float32),
        ],
        scratch_shapes=[pltpu.VMEM((length // BLOCK, 8, BLOCK), jnp.float32)],
        compiler_params=pltpu.CompilerParams(vmem_limit_bytes=48 * 1024 * 1024),
    )(streams, taps, columns)
    across = lax.axis_size("ch")
    dma = pltpu.SemaphoreType.DMA
    return pl.pallas_call(
        functools.partial(send, total_channels),
        in_specs=[pl.BlockSpec(memory_space=pltpu.VMEM)] * 2,
        out_specs=pl.BlockSpec(memory_space=pl.ANY),
        out_shape=jax.ShapeDtypeStruct((owners * channels, own), jnp.bfloat16),
        scratch_shapes=[
            pltpu.VMEM((across, owners, own), jnp.float32),
            pltpu.VMEM((owners, own), jnp.float32),
            pltpu.VMEM((owners, owners, own), jnp.float32),
            pltpu.VMEM((owners, channels, own), jnp.bfloat16),
            pltpu.VMEM((owners, own), jnp.float32),
            dma((across,)),
            dma((across,)),
            dma((owners,)),
            dma((owners,)),
            dma((owners,)),
            dma((owners,)),
            dma,
        ],
        compiler_params=pltpu.CompilerParams(
            collective_id=0, has_side_effects=True, vmem_limit_bytes=24 * 1024 * 1024
        ),
    )(sums, gated)


def solution(mesh):
    placed = (
        P(None, ("ch", "ctx"), None),
        P(None, "ch", None),
        P("ch", None),
        P("ch", None),
        P("ch"),
        P("ch"),
    )

    def whole(streams, *others):
        return jax.shard_map(
            functools.partial(shards, streams.shape[1]),
            mesh=mesh,
            in_specs=placed,
            out_specs=P("ch", "ctx"),
            check_vma=False,
        )(streams, *others)

    return whole
```

```python
import functools

import jax
import jax.numpy as jnp
from jax import lax
from jax.experimental import pallas as pl
from jax.experimental.pallas import tpu as pltpu
from jax.sharding import PartitionSpec as P

BLOCK = 128
MESH = pl.DeviceIdType.MESH


def split(value):
    high = value.astype(jnp.bfloat16)
    low = (value - high.astype(jnp.float32)).astype(jnp.bfloat16)
    return high, low


def halves(array):
    return array[:, :BLOCK] + array[:, BLOCK:]


def rolled(row):
    return pltpu.roll(
        jnp.broadcast_to(row, (BLOCK, BLOCK)), 0, 1, stride=1, stride_axis=0
    )


def column_of(row):
    shape = (row.shape[1], row.shape[1])
    diagonal = lax.broadcasted_iota(jnp.int32, shape, 0) == lax.broadcasted_iota(
        jnp.int32, shape, 1
    )
    return jnp.sum(jnp.where(diagonal, row, 0.0), axis=1, keepdims=True)


def causal_mask():
    shape = (BLOCK, BLOCK)
    return lax.broadcasted_iota(jnp.int32, shape, 1) >= lax.broadcasted_iota(jnp.int32, shape, 0)


def short_weights(taps_row):
    row = jnp.concatenate(
        [taps_row, jnp.zeros((1, BLOCK - taps_row.shape[1]), jnp.float32)], axis=1
    )
    table = rolled(row)
    causal = causal_mask()
    high_now, low_now = split(jnp.where(causal, table, 0.0))
    high_before, low_before = split(jnp.where(causal, 0.0, table))
    return jnp.concatenate(
        [
            jnp.concatenate([high_before, low_before], axis=1),
            jnp.concatenate([high_now, low_now], axis=1),
        ],
        axis=0,
    )


def short_filtered(window, m, rows, chosen, weights):
    def block_at(n):
        return window[m, rows, n * BLOCK : (n + 1) * BLOCK]

    now = jnp.concatenate([block_at(n) for n in chosen], axis=0)
    before = jnp.concatenate(
        [block_at(n - 1) if n else jnp.zeros_like(block_at(0)) for n in chosen], axis=0
    )
    both = jnp.concatenate([before, now], axis=1)
    return halves(jnp.dot(both, weights, preferred_element_type=jnp.float32))


def fused(
    total_channels,
    at_once,
    streams,
    taps,
    pole_rates,
    residues_of,
    skips,
    gains,
    out,
    window,
    gated_at,
    filters,
    tables,
    lifts,
    pairs,
    starts_at,
    squares,
    across,
    column,
    along,
    scales,
    staged,
    fetched,
    across_sent,
    across_got,
    along_sent,
    along_got,
    block_sent,
    block_got,
    kept,
):
    chunks, owners, channels, _ = gated_at.shape
    width = skips.shape[1]
    groups = channels // width
    steps = groups // at_once
    blocks = window.shape[2] // BLOCK
    across_count = lax.axis_size("ch")
    me = lax.axis_index("ctx")
    my_ch = lax.axis_index("ch")
    first_group = me * groups

    def fetch(step):
        rows = pl.ds(pl.multiple_of(step * (at_once * width), 16), at_once * width)
        return pltpu.make_async_copy(
            streams.at[:, rows, :], window.at[:, rows, :], fetched.at[step]
        )

    @pl.loop(0, steps)
    def _(step):
        fetch(step).start()

    def peer_ctx(by):
        return {"ctx": lax.rem(me + by, owners)}

    def peer_ch(by):
        return {"ch": lax.rem(my_ch + by, across_count)}

    barrier = pltpu.get_barrier_semaphore()

    @pl.loop(1, across_count)
    def _(by):
        pl.semaphore_signal(barrier, inc=1, device_id=peer_ch(by), device_id_type=MESH)

    @pl.loop(1, owners)
    def _(by):
        pl.semaphore_signal(barrier, inc=1, device_id=peer_ctx(by), device_id_type=MESH)

    def rows_of(group):
        return pl.ds(pl.multiple_of(group * width, 16), width)

    def finish(group, chunk, pair, starts):
        chosen = range(chunk, blocks, chunks)
        value = short_filtered(window, 0, rows_of(group), chosen, filters[group])
        summed = jnp.dot(pair, tables[group], preferred_element_type=jnp.float32)
        summed += jnp.dot(starts, lifts[group], preferred_element_type=jnp.float32)
        skip = column_of(skips[pl.ds(first_group + group, 1), :])
        gain = column_of(gains[pl.ds(first_group + group, 1), :])
        shaped = (owners, width, BLOCK)
        product = halves(pair.astype(jnp.float32)).reshape(shaped)
        gated = value.reshape(shaped) * (halves(summed).reshape(shaped) + skip[None] * product)
        gated_at[chunk, :, rows_of(group), :] = gated * gain[None]
        return jnp.sum((gated * gated).reshape(owners, width // 8, 8, BLOCK), axis=1)

    def begin(group):
        row = pl.ds(first_group + group, 1)
        filters[group] = short_weights(taps[0, row, :])
        product = 1.0
        for m in (1, 2):
            product *= short_filtered(
                window, m, rows_of(group), range(blocks), short_weights(taps[m, row, :])
            )
        high, low = split(product)
        pair = jnp.concatenate([high, low], axis=1)

        rates = column_of(pole_rates[row, :])
        residues = column_of(residues_of[row, :])
        lags = lax.broadcasted_iota(jnp.int32, (width, BLOCK), 1).astype(jnp.float32)
        modes = residues * jnp.exp(-rates * lags)
        table_high, table_low = split(
            jnp.where(causal_mask(), rolled(jnp.sum(modes, axis=0, keepdims=True)), 0.0)
        )
        table_row = jnp.concatenate([table_high, table_low], axis=1)
        tables[group] = jnp.concatenate([table_row, table_row], axis=0)
        lift_high, lift_low = split(residues * jnp.exp(-rates * (lags + 1.0)))
        lift_row = jnp.concatenate([lift_high, lift_low], axis=1)
        lifts[group] = jnp.concatenate([lift_row, lift_row], axis=0)

        back_high, back_low = split(jnp.exp(-rates * (BLOCK - 1 - lags)))
        back = jnp.concatenate(
            [
                jnp.concatenate([back_high, back_high], axis=1),
                jnp.concatenate([back_low, back_low], axis=1),
            ],
            axis=0,
        )
        ends = lax.dot_general(
            back, pair, (((1,), (1,)), ((), ())), preferred_element_type=jnp.float32
        )
        states = ends[:width] + ends[width:]
        lane = lax.broadcasted_iota(jnp.int32, states.shape, 1)
        reach = 1
        while reach < blocks:
            earlier = pltpu.roll(states, reach * width, 1)
            decay = jnp.exp(-rates * (BLOCK * reach))
            states = states + jnp.where(lane >= reach * width, decay * earlier, 0.0)
            reach *= 2
        starts = jnp.where(lane >= width, pltpu.roll(states, width, 1), 0.0)
        starts_high, starts_low = split(starts)
        starts = jnp.concatenate(
            [starts_high.astype(jnp.float32), starts_low.astype(jnp.float32)], axis=0
        ).T.astype(jnp.bfloat16)

        def of_chunk(array, chunk):
            return jnp.concatenate(
                [array[n * width : (n + 1) * width] for n in range(chunk, blocks, chunks)], axis=0
            )

        for chunk in range(1, chunks):
            pairs[chunk - 1, group] = of_chunk(pair, chunk)
            starts_at[chunk - 1, group] = of_chunk(starts, chunk)
        return of_chunk(pair, 0), of_chunk(starts, 0)

    squares[...] = jnp.zeros_like(squares)

    @pl.loop(0, steps)
    def _(step):
        fetch(step).wait()
        begun = [begin(step * at_once + i) for i in range(at_once)]
        for i, held in enumerate(begun):
            squares[0] += finish(step * at_once + i, 0, *held)

    def later(chunk, low, high):
        @pl.loop(low, high)
        def _(step):
            total = 0.0
            for i in range(at_once):
                group = step * at_once + i
                total += finish(
                    group, chunk, pairs[chunk - 1, group], starts_at[chunk - 1, group]
                )
            squares[chunk] += total

    def across_copy(chunk, by):
        return pltpu.make_async_remote_copy(
            src_ref=across.at[chunk, 0],
            dst_ref=across.at[chunk, by],
            send_sem=across_sent.at[chunk, by],
            recv_sem=across_got.at[chunk, by],
            device_id=peer_ch(by),
            device_id_type=MESH,
        )

    def along_copy(chunk, by):
        return pltpu.make_async_remote_copy(
            src_ref=column.at[chunk],
            dst_ref=along.at[chunk, by],
            send_sem=along_sent.at[chunk, by],
            recv_sem=along_got.at[chunk, by],
            device_id=peer_ctx(by),
            device_id_type=MESH,
        )

    def place(chunk, owner):
        return out.at[
            pl.ds(pl.multiple_of(owner * channels, 16), channels),
            chunk * BLOCK : (chunk + 1) * BLOCK,
        ]

    def block_copy(chunk, by, owner):
        return pltpu.make_async_remote_copy(
            src_ref=staged.at[chunk, by],
            dst_ref=place(chunk, owner),
            send_sem=block_sent.at[chunk, by],
            recv_sem=block_got.at[chunk, by],
            device_id=peer_ctx(by),
            device_id_type=MESH,
        )

    def start_across(chunk):
        across[chunk, 0] = jnp.sum(squares[chunk], axis=1)

        @pl.loop(1, across_count)
        def _(by):
            across_copy(chunk, by).start()

    def start_along(chunk):
        @pl.loop(1, across_count)
        def _(by):
            across_copy(chunk, by).wait()

        column[chunk] = jnp.sum(across[chunk], axis=0)

        @pl.loop(1, owners)
        def _(by):
            along_copy(chunk, by).start()

    def start_blocks(chunk):
        along[chunk, 0] = column[chunk]

        @pl.loop(1, owners)
        def _(by):
            along_copy(chunk, by).wait()

        total = jnp.sum(along[chunk], axis=0)
        scales[chunk] = lax.rsqrt(total / total_channels + 1e-05)

        def fill(by):
            target = lax.rem(me + by, owners)
            row = scales[chunk, pl.ds(target, 1), :]
            staged[chunk, by] = (gated_at[chunk, target] * row).astype(jnp.bfloat16)

        @pl.loop(1, owners)
        def _(by):
            fill(by)
            block_copy(chunk, by, me).start()

        fill(0)
        pltpu.make_async_copy(staged.at[chunk, 0], place(chunk, me), kept.at[chunk]).start()

    def wait_blocks(chunk):
        pltpu.make_async_copy(staged.at[chunk, 0], place(chunk, me), kept.at[chunk]).wait()

        @pl.loop(1, owners)
        def _(by):
            block_copy(chunk, by, me).wait_send()
            block_copy(chunk, by, lax.rem(me + owners - by, owners)).wait_recv()

    pl.semaphore_wait(barrier, across_count + owners - 2)
    cuts = (0, (3 * steps) // 8, (6 * steps) // 8, steps)
    for chunk in range(chunks):
        more = chunk + 1 < chunks
        start_across(chunk)
        if more:
            later(chunk + 1, cuts[0], cuts[1])
        start_along(chunk)
        if more:
            later(chunk + 1, cuts[1], cuts[2])
        start_blocks(chunk)
        if more:
            later(chunk + 1, cuts[2], cuts[3])
    for chunk in range(chunks):
        wait_blocks(chunk)


def shards(total_channels, streams, short_taps, pole_rates, residues, skip, gain):
    owners = lax.axis_size("ctx")
    across = lax.axis_size("ch")
    channels, length = streams.shape[1:]
    groups = pole_rates.shape[0] // owners
    width = channels // groups
    assert pole_rates.shape[1] == width
    own = length // owners
    chunks = own // BLOCK
    later = max(chunks - 1, 1)
    at_once = 2 if groups % 2 == 0 else 1
    vmem = pltpu.VMEM
    dma = pltpu.SemaphoreType.DMA
    f32 = jnp.float32
    bf16 = jnp.bfloat16
    return pl.pallas_call(
        functools.partial(fused, total_channels, at_once),
        in_specs=[pl.BlockSpec(memory_space=pl.ANY)] + [pl.BlockSpec(memory_space=vmem)] * 5,
        out_specs=pl.BlockSpec(memory_space=pl.ANY),
        out_shape=jax.ShapeDtypeStruct((owners * channels, own), bf16),
        scratch_shapes=[
            vmem(streams.shape, bf16),
            vmem((chunks, owners, channels, BLOCK), f32),
            vmem((groups, 2 * BLOCK, 2 * BLOCK), bf16),
            vmem((groups, 2 * BLOCK, 2 * BLOCK), bf16),
            vmem((groups, 2 * width, 2 * BLOCK), bf16),
            vmem((later, groups, owners * width, 2 * BLOCK), bf16),
            vmem((later, groups, owners * width, 2 * width), bf16),
            vmem((chunks, owners, 8, BLOCK), f32),
            vmem((chunks, across, owners, BLOCK), f32),
            vmem((chunks, owners, BLOCK), f32),
            vmem((chunks, owners, owners, BLOCK), f32),
            vmem((chunks, owners, BLOCK), f32),
            vmem((chunks, owners, channels, BLOCK), bf16),
            dma((groups // at_once,)),
            dma((chunks, across)),
            dma((chunks, across)),
            dma((chunks, owners)),
            dma((chunks, owners)),
            dma((chunks, owners)),
            dma((chunks, owners)),
            dma((chunks,)),
        ],
        compiler_params=pltpu.CompilerParams(
            collective_id=0, has_side_effects=True, vmem_limit_bytes=56 * 1024 * 1024
        ),
    )(
        streams,
        short_taps,
        pole_rates,
        residues,
        skip.reshape(-1, width),
        gain.reshape(-1, width),
    )


def solution(mesh):
    placed = (
        P(None, ("ch", "ctx"), None),
        P(None, "ch", None),
        P("ch", None),
        P("ch", None),
        P("ch"),
        P("ch"),
    )

    def whole(streams, *others):
        return jax.shard_map(
            functools.partial(shards, streams.shape[1]),
            mesh=mesh,
            in_specs=placed,
            out_specs=P("ch", "ctx"),
            check_vma=False,
        )(streams, *others)

    return whole
```

```python
import functools

import jax
import jax.numpy as jnp
from jax import lax
from jax.experimental import pallas as pl
from jax.experimental.pallas import tpu as pltpu
from jax.sharding import PartitionSpec as P

BLOCK = 128
MESH = pl.DeviceIdType.MESH


def split(value):
    high = value.astype(jnp.bfloat16)
    low = (value - high.astype(jnp.float32)).astype(jnp.bfloat16)
    return high, low


def halves(array):
    return array[:, :BLOCK] + array[:, BLOCK:]


def rolled(row):
    return pltpu.roll(
        jnp.broadcast_to(row, (BLOCK, BLOCK)), 0, 1, stride=1, stride_axis=0
    )


def picked(array, lane):
    lanes = lax.broadcasted_iota(jnp.int32, array.shape, 1)
    return jnp.sum(jnp.where(lanes == lane, array, 0.0), axis=1, keepdims=True)


def upright(row, offset, width):
    shape = (width, row.shape[1])
    lane = lax.broadcasted_iota(jnp.int32, shape, 1)
    at = lax.broadcasted_iota(jnp.int32, shape, 0) + offset
    return jnp.sum(jnp.where(lane == at, row, 0.0), axis=1, keepdims=True)


def flat(column):
    shape = (column.shape[0], BLOCK)
    diagonal = lax.broadcasted_iota(jnp.int32, shape, 0) == lax.broadcasted_iota(
        jnp.int32, shape, 1
    )
    return jnp.sum(jnp.where(diagonal, column, 0.0), axis=0, keepdims=True)


def causal_mask():
    shape = (BLOCK, BLOCK)
    row = lax.broadcasted_iota(jnp.int32, shape, 0)
    lane = lax.broadcasted_iota(jnp.int32, shape, 1)
    return jnp.where(lane >= row, 1.0, 0.0).astype(jnp.bfloat16)


def short_weights(taps_column, causal):
    high, low = split(rolled(flat(taps_column)))
    now = jnp.concatenate([high * causal, low * causal], axis=1)
    before = jnp.concatenate([high, low], axis=1) - now
    return jnp.concatenate([before, now], axis=0)


def short_filtered(window, m, rows, chosen, weights):
    def block_at(n):
        return window[m, rows, n * BLOCK : (n + 1) * BLOCK]

    now = jnp.concatenate([block_at(n) for n in chosen], axis=0)
    before = jnp.concatenate(
        [block_at(n - 1) if n else jnp.zeros_like(block_at(0)) for n in chosen], axis=0
    )
    both = jnp.concatenate([before, now], axis=1)
    return halves(jnp.dot(both, weights, preferred_element_type=jnp.float32))


def fused(
    total_channels,
    at_once,
    streams,
    taps,
    pole_rates,
    residues_of,
    skips,
    gains,
    out,
    window,
    gated_at,
    filters,
    tables,
    held_at,
    squares,
    sums,
    scales,
    staged,
    fetched,
    sums_sent,
    sums_got,
    block_sent,
    block_got,
    kept,
):
    chunks, owners, channels, _ = gated_at.shape
    width = pole_rates.shape[0]
    groups = channels // width
    steps = groups // at_once
    blocks = window.shape[2] // BLOCK
    across_count = lax.axis_size("ch")
    me = lax.axis_index("ctx")
    my_ch = lax.axis_index("ch")
    first_group = me * groups

    def fetch(step):
        rows = pl.ds(pl.multiple_of(step * (at_once * width), 16), at_once * width)
        return pltpu.make_async_copy(
            streams.at[:, rows, :], window.at[:, rows, :], fetched.at[step]
        )

    @pl.loop(0, steps)
    def _(step):
        fetch(step).start()

    def peer_ctx(by):
        return {"ctx": lax.rem(me + by, owners)}

    def peer(by):
        return {
            "ctx": lax.rem(me + lax.div(by, across_count), owners),
            "ch": lax.rem(my_ch + lax.rem(by, across_count), across_count),
        }

    devices = owners * across_count
    barrier = pltpu.get_barrier_semaphore()

    @pl.loop(1, devices)
    def _(by):
        pl.semaphore_signal(barrier, inc=1, device_id=peer(by), device_id_type=MESH)

    causal = causal_mask()

    def rows_of(group):
        return pl.ds(pl.multiple_of(group * width, 16), width)

    def per_channel(values, group):
        at = (first_group + group) * width
        return upright(values[pl.ds(lax.div(at, BLOCK), 1), :], lax.rem(at, BLOCK), width)

    def finish(group, chunk, held):
        chosen = range(chunk, blocks, chunks)
        value = short_filtered(window, 0, rows_of(group), chosen, filters[group])
        high, low, starts = (held[:, i * BLOCK : (i + 1) * BLOCK] for i in range(3))
        convolved = jnp.dot(
            jnp.concatenate([high, low, high, starts], axis=1),
            tables[group],
            preferred_element_type=jnp.float32,
        )
        skip = per_channel(skips, group)
        gain = per_channel(gains, group)
        shaped = (owners, width, BLOCK)
        product = (high.astype(jnp.float32) + low.astype(jnp.float32)).reshape(shaped)
        gated = value.reshape(shaped) * (convolved.reshape(shaped) + skip[None] * product)
        gated_at[chunk, :, rows_of(group), :] = gated * gain[None]
        return jnp.sum((gated * gated).reshape(owners, width // 8, 8, BLOCK), axis=1)

    def begin(group):
        at = first_group + group
        filters[group] = short_weights(picked(taps[0], at), causal)
        product = 1.0
        for m in (1, 2):
            product *= short_filtered(
                window, m, rows_of(group), range(blocks), short_weights(picked(taps[m], at), causal)
            )
        high, low = split(product)
        pair = jnp.concatenate([high, low], axis=1)

        rates = picked(pole_rates[...], at)
        residues = picked(residues_of[...], at)
        lags = lax.broadcasted_iota(jnp.int32, (width, BLOCK), 1).astype(jnp.float32)
        modes = residues * jnp.exp(-rates * lags)
        table_high, table_low = split(rolled(jnp.sum(modes, axis=0, keepdims=True)))
        table_high = table_high * causal
        lift_high, lift_low = split(residues * jnp.exp(-rates * (lags + 1.0)))
        spare = BLOCK - 3 * width
        tables[group] = jnp.concatenate(
            [
                table_high,
                table_high,
                table_low * causal,
                lift_high,
                lift_high,
                lift_low,
                jnp.zeros((spare, BLOCK), jnp.bfloat16),
            ],
            axis=0,
        )

        back_high, back_low = split(jnp.exp(-rates * (BLOCK - 1 - lags)))
        back = jnp.concatenate(
            [
                jnp.concatenate([back_high, back_high], axis=1),
                jnp.concatenate([back_low, back_low], axis=1),
            ],
            axis=0,
        )
        ends = lax.dot_general(
            back, pair, (((1,), (1,)), ((), ())), preferred_element_type=jnp.float32
        )
        states = ends[:width] + ends[width:]
        lane = lax.broadcasted_iota(jnp.int32, states.shape, 1)
        reach = 1
        while reach < blocks:
            earlier = pltpu.roll(states, reach * width, 1)
            decay = jnp.exp(-rates * (BLOCK * reach))
            states = states + jnp.where(lane >= reach * width, decay * earlier, 0.0)
            reach *= 2
        starts = jnp.where(lane >= width, pltpu.roll(states, width, 1), 0.0)
        starts_high, starts_low = (part.astype(jnp.float32) for part in split(starts))
        starts = jnp.concatenate(
            [
                starts_high,
                starts_low,
                starts_high,
                jnp.zeros((spare, starts.shape[1]), jnp.float32),
            ],
            axis=0,
        ).T.astype(jnp.bfloat16)
        held = jnp.concatenate([pair, starts], axis=1)

        def of_chunk(chunk):
            return jnp.concatenate(
                [held[n * width : (n + 1) * width] for n in range(chunk, blocks, chunks)], axis=0
            )

        for chunk in range(1, chunks):
            held_at[chunk - 1, group] = of_chunk(chunk)
        return of_chunk(0)

    squares[...] = jnp.zeros_like(squares)

    @pl.loop(0, steps)
    def _(step):
        fetch(step).wait()
        begun = [begin(step * at_once + i) for i in range(at_once)]
        for i, held in enumerate(begun):
            squares[0] += finish(step * at_once + i, 0, held)

    def later(chunk, low, high):
        @pl.loop(low, high)
        def _(step):
            total = 0.0
            for i in range(at_once):
                group = step * at_once + i
                total += finish(group, chunk, held_at[chunk - 1, group])
            squares[chunk] += total

    def sums_copy(chunk, by):
        return pltpu.make_async_remote_copy(
            src_ref=sums.at[chunk, 0],
            dst_ref=sums.at[chunk, by],
            send_sem=sums_sent.at[chunk, by],
            recv_sem=sums_got.at[chunk, by],
            device_id=peer(by),
            device_id_type=MESH,
        )

    def place(chunk, owner):
        return out.at[
            pl.ds(pl.multiple_of(owner * channels, 16), channels),
            chunk * BLOCK : (chunk + 1) * BLOCK,
        ]

    def block_copy(chunk, by, owner):
        return pltpu.make_async_remote_copy(
            src_ref=staged.at[chunk, by],
            dst_ref=place(chunk, owner),
            send_sem=block_sent.at[chunk, by],
            recv_sem=block_got.at[chunk, by],
            device_id=peer_ctx(by),
            device_id_type=MESH,
        )

    def start_sums(chunk):
        sums[chunk, 0] = jnp.sum(squares[chunk], axis=1)

        @pl.loop(1, devices)
        def _(by):
            sums_copy(chunk, by).start()

    def start_blocks(chunk):
        @pl.loop(1, devices)
        def _(by):
            sums_copy(chunk, by).wait()

        total = jnp.sum(sums[chunk], axis=0)
        scales[chunk] = lax.rsqrt(total / total_channels + 1e-05)

        def fill(by):
            target = lax.rem(me + by, owners)
            row = scales[chunk, pl.ds(target, 1), :]
            staged[chunk, by] = (gated_at[chunk, target] * row).astype(jnp.bfloat16)

        @pl.loop(1, owners)
        def _(by):
            fill(by)
            block_copy(chunk, by, me).start()

        fill(0)
        pltpu.make_async_copy(staged.at[chunk, 0], place(chunk, me), kept.at[chunk]).start()

    def wait_blocks(chunk):
        pltpu.make_async_copy(staged.at[chunk, 0], place(chunk, me), kept.at[chunk]).wait()

        @pl.loop(1, owners)
        def _(by):
            block_copy(chunk, by, me).wait_send()
            block_copy(chunk, by, lax.rem(me + owners - by, owners)).wait_recv()

    pl.semaphore_wait(barrier, devices - 1)
    start_sums(0)
    for chunk in range(chunks):
        if chunk + 1 < chunks:
            later(chunk + 1, 0, steps)
            start_sums(chunk + 1)
        start_blocks(chunk)
    for chunk in range(chunks):
        wait_blocks(chunk)


def shards(total_channels, streams, short_taps, pole_rates, residues, skip, gain):
    owners = lax.axis_size("ctx")
    across = lax.axis_size("ch")
    channels, length = streams.shape[1:]
    groups = pole_rates.shape[0] // owners
    width = channels // groups
    assert pole_rates.shape[1] == width
    own = length // owners
    chunks = own // BLOCK
    later = max(chunks - 1, 1)
    devices = owners * across
    at_once = 2 if groups % 2 == 0 else 1
    vmem = pltpu.VMEM
    dma = pltpu.SemaphoreType.DMA
    f32 = jnp.float32
    bf16 = jnp.bfloat16
    return pl.pallas_call(
        functools.partial(fused, total_channels, at_once),
        in_specs=[pl.BlockSpec(memory_space=pltpu.HBM)] + [pl.BlockSpec(memory_space=vmem)] * 5,
        out_specs=pl.BlockSpec(memory_space=pl.ANY),
        out_shape=jax.ShapeDtypeStruct((owners * channels, own), bf16),
        scratch_shapes=[
            vmem(streams.shape, bf16),
            vmem((chunks, owners, channels, BLOCK), f32),
            vmem((groups, 2 * BLOCK, 2 * BLOCK), bf16),
            vmem((groups, 4 * BLOCK, BLOCK), bf16),
            vmem((later, groups, owners * width, 3 * BLOCK), bf16),
            vmem((chunks, owners, 8, BLOCK), f32),
            vmem((chunks, devices, owners, BLOCK), f32),
            vmem((chunks, owners, BLOCK), f32),
            vmem((chunks, owners, channels, BLOCK), bf16),
            dma((groups // at_once,)),
            dma((chunks, devices)),
            dma((chunks, devices)),
            dma((chunks, owners)),
            dma((chunks, owners)),
            dma((chunks,)),
        ],
        compiler_params=pltpu.CompilerParams(
            collective_id=0, has_side_effects=True, vmem_limit_bytes=40 * 1024 * 1024
        ),
    )(
        streams,
        short_taps.transpose(0, 2, 1),
        pole_rates.T,
        residues.T,
        skip.reshape(-1, BLOCK),
        gain.reshape(-1, BLOCK),
    )


def solution(mesh):
    placed = (
        P(None, ("ch", "ctx"), None),
        P(None, "ch", None),
        P("ch", None),
        P("ch", None),
        P("ch"),
        P("ch"),
    )

    def whole(streams, *others):
        return jax.shard_map(
            functools.partial(shards, streams.shape[1]),
            mesh=mesh,
            in_specs=placed,
            out_specs=P("ch", "ctx"),
            check_vma=False,
        )(streams, *others)

    return whole
```

```python
import functools

import jax
import jax.numpy as jnp
from jax import lax
from jax.experimental import pallas as pl
from jax.experimental.pallas import tpu as pltpu
from jax.sharding import PartitionSpec as P

BLOCK = 128
MESH = pl.DeviceIdType.MESH


def split(value):
    high = value.astype(jnp.bfloat16)
    low = (value - high.astype(jnp.float32)).astype(jnp.bfloat16)
    return high, low


def halves(array):
    return array[:, :BLOCK] + array[:, BLOCK:]


def rolled(row):
    return pltpu.roll(
        jnp.broadcast_to(row, (BLOCK, BLOCK)), 0, 1, stride=1, stride_axis=0
    )


def picked(array, lane):
    lanes = lax.broadcasted_iota(jnp.int32, array.shape, 1)
    return jnp.sum(jnp.where(lanes == lane, array, 0.0), axis=1, keepdims=True)


def upright(row, offset, width):
    shape = (width, row.shape[1])
    lane = lax.broadcasted_iota(jnp.int32, shape, 1)
    at = lax.broadcasted_iota(jnp.int32, shape, 0) + offset
    return jnp.sum(jnp.where(lane == at, row, 0.0), axis=1, keepdims=True)


def flat(column):
    shape = (column.shape[0], BLOCK)
    diagonal = lax.broadcasted_iota(jnp.int32, shape, 0) == lax.broadcasted_iota(
        jnp.int32, shape, 1
    )
    return jnp.sum(jnp.where(diagonal, column, 0.0), axis=0, keepdims=True)


def causal_mask():
    shape = (BLOCK, BLOCK)
    row = lax.broadcasted_iota(jnp.int32, shape, 0)
    lane = lax.broadcasted_iota(jnp.int32, shape, 1)
    return jnp.where(lane >= row, 1.0, 0.0).astype(jnp.bfloat16)


def short_weights(taps_column, causal):
    high, low = split(rolled(flat(taps_column)))
    now = jnp.concatenate([high * causal, low * causal], axis=1)
    before = jnp.concatenate([high, low], axis=1) - now
    return jnp.concatenate([before, now], axis=0)


def short_filtered(window, m, rows, chosen, weights):
    def block_at(n):
        return window[m, rows, n * BLOCK : (n + 1) * BLOCK]

    now = jnp.concatenate([block_at(n) for n in chosen], axis=0)
    before = jnp.concatenate(
        [block_at(n - 1) if n else jnp.zeros_like(block_at(0)) for n in chosen], axis=0
    )
    both = jnp.concatenate([before, now], axis=1)
    return halves(jnp.dot(both, weights, preferred_element_type=jnp.float32))


def settle(source, target, copied):
    count = copied.shape[0]
    height = source.shape[0] // count

    def piece(i):
        rows = pl.ds(i * height, height)
        return pltpu.make_async_copy(source.at[rows, :], target.at[rows, :], copied.at[i])

    for i in range(count):
        piece(i).start()
    for i in range(count):
        piece(i).wait()


def fused(
    total_channels,
    at_once,
    early_steps,
    streams,
    taps,
    pole_rates,
    residues_of,
    skips,
    gains,
    out,
    window,
    gated_at,
    filters,
    tables,
    held_at,
    squares,
    sums,
    scales,
    staged,
    early,
    early_staged,
    fetched,
    early_sent,
    early_got,
    early_kept,
    sums_sent,
    sums_got,
    block_sent,
    block_got,
    kept,
):
    chunks, owners, channels, _ = gated_at.shape
    width = pole_rates.shape[0]
    groups = channels // width
    steps = groups // at_once
    blocks = window.shape[2] // BLOCK
    across_count = lax.axis_size("ch")
    me = lax.axis_index("ctx")
    my_ch = lax.axis_index("ch")
    first_group = me * groups

    def fetch(step):
        rows = pl.ds(pl.multiple_of(step * (at_once * width), 16), at_once * width)
        return pltpu.make_async_copy(
            streams.at[:, rows, :], window.at[:, rows, :], fetched.at[step]
        )

    @pl.loop(0, steps)
    def _(step):
        fetch(step).start()

    def peer_ctx(by):
        return {"ctx": lax.rem(me + by, owners)}

    def peer(by):
        return {
            "ctx": lax.rem(me + lax.div(by, across_count), owners),
            "ch": lax.rem(my_ch + lax.rem(by, across_count), across_count),
        }

    devices = owners * across_count
    barrier = pltpu.get_barrier_semaphore()

    @pl.loop(1, devices)
    def _(by):
        pl.semaphore_signal(barrier, inc=1, device_id=peer(by), device_id_type=MESH)

    causal = causal_mask()

    def rows_of(group):
        return pl.ds(pl.multiple_of(group * width, 16), width)

    def per_channel(values, group):
        at = (first_group + group) * width
        return upright(values[pl.ds(lax.div(at, BLOCK), 1), :], lax.rem(at, BLOCK), width)

    def finish(group, chunk, held):
        chosen = range(chunk, blocks, chunks)
        value = short_filtered(window, 0, rows_of(group), chosen, filters[group])
        high, low, starts = (held[:, i * BLOCK : (i + 1) * BLOCK] for i in range(3))
        convolved = jnp.dot(
            jnp.concatenate([high, low, high, starts], axis=1),
            tables[group],
            preferred_element_type=jnp.float32,
        )
        skip = per_channel(skips, group)
        gain = per_channel(gains, group)
        shaped = (owners, width, BLOCK)
        product = (high.astype(jnp.float32) + low.astype(jnp.float32)).reshape(shaped)
        gated = value.reshape(shaped) * (convolved.reshape(shaped) + skip[None] * product)
        gated_at[chunk, :, rows_of(group), :] = gated * gain[None]
        return jnp.sum((gated * gated).reshape(owners, width // 8, 8, BLOCK), axis=1)

    def begin(group):
        at = first_group + group
        filters[group] = short_weights(picked(taps[0], at), causal)
        product = 1.0
        for m in (1, 2):
            product *= short_filtered(
                window, m, rows_of(group), range(blocks), short_weights(picked(taps[m], at), causal)
            )
        high, low = split(product)
        pair = jnp.concatenate([high, low], axis=1)

        rates = picked(pole_rates[...], at)
        residues = picked(residues_of[...], at)
        lags = lax.broadcasted_iota(jnp.int32, (width, BLOCK), 1).astype(jnp.float32)
        modes = residues * jnp.exp(-rates * lags)
        table_high, table_low = split(rolled(jnp.sum(modes, axis=0, keepdims=True)))
        table_high = table_high * causal
        lift_high, lift_low = split(residues * jnp.exp(-rates * (lags + 1.0)))
        spare = BLOCK - 3 * width
        tables[group] = jnp.concatenate(
            [
                table_high,
                table_high,
                table_low * causal,
                lift_high,
                lift_high,
                lift_low,
                jnp.zeros((spare, BLOCK), jnp.bfloat16),
            ],
            axis=0,
        )

        back_high, back_low = split(jnp.exp(-rates * (BLOCK - 1 - lags)))
        back = jnp.concatenate(
            [
                jnp.concatenate([back_high, back_high], axis=1),
                jnp.concatenate([back_low, back_low], axis=1),
            ],
            axis=0,
        )
        ends = lax.dot_general(
            back, pair, (((1,), (1,)), ((), ())), preferred_element_type=jnp.float32
        )
        states = ends[:width] + ends[width:]
        lane = lax.broadcasted_iota(jnp.int32, states.shape, 1)
        reach = 1
        while reach < blocks:
            earlier = pltpu.roll(states, reach * width, 1)
            decay = jnp.exp(-rates * (BLOCK * reach))
            states = states + jnp.where(lane >= reach * width, decay * earlier, 0.0)
            reach *= 2
        starts = jnp.where(lane >= width, pltpu.roll(states, width, 1), 0.0)
        starts_high, starts_low = (part.astype(jnp.float32) for part in split(starts))
        starts = jnp.concatenate(
            [
                starts_high,
                starts_low,
                starts_high,
                jnp.zeros((spare, starts.shape[1]), jnp.float32),
            ],
            axis=0,
        ).T.astype(jnp.bfloat16)
        held = jnp.concatenate([pair, starts], axis=1)

        def of_chunk(chunk):
            return jnp.concatenate(
                [held[n * width : (n + 1) * width] for n in range(chunk, blocks, chunks)], axis=0
            )

        for chunk in range(1, chunks):
            held_at[chunk - 1, group] = of_chunk(chunk)
        return of_chunk(0)

    early_channels = early_steps * at_once * width

    def early_copy(step, by):
        rows = pl.ds(pl.multiple_of(step * (at_once * width), 16), at_once * width)
        return pltpu.make_async_remote_copy(
            src_ref=gated_at.at[0, lax.rem(me + by, owners), rows, :],
            dst_ref=early.at[by, rows, :],
            send_sem=early_sent.at[step, by],
            recv_sem=early_got.at[step, by],
            device_id=peer_ctx(by),
            device_id_type=MESH,
        )

    def early_keep(by):
        source = lax.rem(me + owners - by, owners)
        return pltpu.make_async_copy(
            early_staged.at[by],
            out.at[pl.ds(pl.multiple_of(source * channels, 16), early_channels), :BLOCK],
            early_kept.at[by],
        )

    def keep_early():
        @pl.loop(1, owners)
        def _(by):
            for step in range(early_steps):
                early_copy(step, by).wait()
            row = scales[0, pl.ds(me, 1), :]
            early_staged[by] = (early[by] * row).astype(jnp.bfloat16)
            early_keep(by).start()

    squares[...] = jnp.zeros_like(squares)

    @pl.loop(0, steps)
    def _(step):
        fetch(step).wait()
        begun = [begin(step * at_once + i) for i in range(at_once)]
        for i, held in enumerate(begun):
            squares[0] += finish(step * at_once + i, 0, held)

        if early_steps:

            @pl.when(step == 0)
            def _():
                pl.semaphore_wait(barrier, devices - 1)

            @pl.when(step < early_steps)
            def _():
                @pl.loop(1, owners)
                def _(by):
                    early_copy(step, by).start()

    def later(chunk, low, high):
        @pl.loop(low, high)
        def _(step):
            total = 0.0
            for i in range(at_once):
                group = step * at_once + i
                total += finish(group, chunk, held_at[chunk - 1, group])
            squares[chunk] += total

    def sums_copy(chunk, by):
        return pltpu.make_async_remote_copy(
            src_ref=sums.at[chunk, 0],
            dst_ref=sums.at[chunk, by],
            send_sem=sums_sent.at[chunk, by],
            recv_sem=sums_got.at[chunk, by],
            device_id=peer(by),
            device_id_type=MESH,
        )

    def place(chunk, owner, first):
        return out.at[
            pl.ds(pl.multiple_of(owner * channels + first, 16), channels - first),
            chunk * BLOCK : (chunk + 1) * BLOCK,
        ]

    def first_of(chunk):
        return early_channels if chunk == 0 else 0

    def block_copy(chunk, by, owner):
        first = first_of(chunk)
        return pltpu.make_async_remote_copy(
            src_ref=staged.at[chunk, by, first:, :],
            dst_ref=place(chunk, owner, first),
            send_sem=block_sent.at[chunk, by],
            recv_sem=block_got.at[chunk, by],
            device_id=peer_ctx(by),
            device_id_type=MESH,
        )

    def own_copy(chunk):
        return pltpu.make_async_copy(
            staged.at[chunk, 0], place(chunk, me, 0), kept.at[chunk]
        )

    def start_sums(chunk):
        sums[chunk, 0] = jnp.sum(squares[chunk], axis=1)

        @pl.loop(1, devices)
        def _(by):
            sums_copy(chunk, by).start()

    def start_blocks(chunk):
        @pl.loop(1, devices)
        def _(by):
            sums_copy(chunk, by).wait()

        total = jnp.sum(sums[chunk], axis=0)
        scales[chunk] = lax.rsqrt(total / total_channels + 1e-05)

        def fill(by, first):
            target = lax.rem(me + by, owners)
            row = scales[chunk, pl.ds(target, 1), :]
            staged[chunk, by, first:, :] = (gated_at[chunk, target, first:, :] * row).astype(
                jnp.bfloat16
            )

        @pl.loop(1, owners)
        def _(by):
            fill(by, first_of(chunk))
            block_copy(chunk, by, me).start()

        fill(0, 0)
        own_copy(chunk).start()

    def wait_blocks(chunk):
        own_copy(chunk).wait()

        @pl.loop(1, owners)
        def _(by):
            block_copy(chunk, by, me).wait_send()
            block_copy(chunk, by, lax.rem(me + owners - by, owners)).wait_recv()

    if not early_steps:
        pl.semaphore_wait(barrier, devices - 1)
    start_sums(0)
    for chunk in range(chunks):
        if chunk + 1 < chunks:
            later(chunk + 1, 0, steps)
            start_sums(chunk + 1)
        start_blocks(chunk)
    if early_steps:
        keep_early()
    for chunk in range(chunks):
        wait_blocks(chunk)
    if early_steps:

        @pl.loop(1, owners)
        def _(by):
            early_keep(by).wait()


def shards(total_channels, streams, short_taps, pole_rates, residues, skip, gain):
    owners = lax.axis_size("ctx")
    across = lax.axis_size("ch")
    channels, length = streams.shape[1:]
    groups = pole_rates.shape[0] // owners
    width = channels // groups
    assert pole_rates.shape[1] == width
    own = length // owners
    chunks = own // BLOCK
    later = max(chunks - 1, 1)
    devices = owners * across
    at_once = next(n for n in (4, 2, 1) if groups % n == 0)
    steps = groups // at_once
    early_steps = steps // 2
    early_channels = max(early_steps, 1) * at_once * width
    vmem = pltpu.VMEM
    dma = pltpu.SemaphoreType.DMA
    f32 = jnp.float32
    bf16 = jnp.bfloat16
    moved = pl.pallas_call(
        functools.partial(fused, total_channels, at_once, early_steps),
        in_specs=[pl.BlockSpec(memory_space=pltpu.HBM)] + [pl.BlockSpec(memory_space=vmem)] * 5,
        out_specs=pl.BlockSpec(memory_space=pl.ANY),
        out_shape=jax.ShapeDtypeStruct((owners * channels, own), bf16),
        scratch_shapes=[
            vmem(streams.shape, bf16),
            vmem((chunks, owners, channels, BLOCK), f32),
            vmem((groups, 2 * BLOCK, 2 * BLOCK), bf16),
            vmem((groups, 4 * BLOCK, BLOCK), bf16),
            vmem((later, groups, owners * width, 3 * BLOCK), bf16),
            vmem((chunks, owners, 8, BLOCK), f32),
            vmem((chunks, devices, owners, BLOCK), f32),
            vmem((chunks, owners, BLOCK), f32),
            vmem((chunks, owners, channels, BLOCK), bf16),
            vmem((owners, early_channels, BLOCK), f32),
            vmem((owners, early_channels, BLOCK), bf16),
            dma((steps,)),
            dma((max(early_steps, 1), owners)),
            dma((max(early_steps, 1), owners)),
            dma((owners,)),
            dma((chunks, devices)),
            dma((chunks, devices)),
            dma((chunks, owners)),
            dma((chunks, owners)),
            dma((chunks,)),
        ],
        compiler_params=pltpu.CompilerParams(
            collective_id=0, has_side_effects=True, vmem_limit_bytes=56 * 1024 * 1024
        ),
    )(
        streams,
        short_taps.transpose(0, 2, 1),
        pole_rates.T,
        residues.T,
        skip.reshape(-1, BLOCK),
        gain.reshape(-1, BLOCK),
    )
    return pl.pallas_call(
        settle,
        in_specs=[pl.BlockSpec(memory_space=pl.ANY)],
        out_specs=pl.BlockSpec(memory_space=pl.ANY),
        out_shape=jax.ShapeDtypeStruct(moved.shape, moved.dtype),
        scratch_shapes=[dma((8,))],
        compiler_params=pltpu.CompilerParams(vmem_limit_bytes=56 * 1024 * 1024),
    )(moved)


def solution(mesh):
    placed = (
        P(None, ("ch", "ctx"), None),
        P(None, "ch", None),
        P("ch", None),
        P("ch", None),
        P("ch"),
        P("ch"),
    )

    def whole(streams, *others):
        return jax.shard_map(
            functools.partial(shards, streams.shape[1]),
            mesh=mesh,
            in_specs=placed,
            out_specs=P("ch", "ctx"),
            check_vma=False,
        )(streams, *others)

    return whole
```

```python
import functools

import jax
import jax.numpy as jnp
from jax import lax
from jax.experimental import pallas as pl
from jax.experimental.pallas import tpu as pltpu
from jax.sharding import PartitionSpec as P

BLOCK = 128
MESH = pl.DeviceIdType.MESH


def split(value):
    high = value.astype(jnp.bfloat16)
    low = (value - high.astype(jnp.float32)).astype(jnp.bfloat16)
    return high, low


def halves(array):
    return array[:, :BLOCK] + array[:, BLOCK:]


def rolled(row):
    return pltpu.roll(
        jnp.broadcast_to(row, (BLOCK, BLOCK)), 0, 1, stride=1, stride_axis=0
    )


def picked(array, lane):
    lanes = lax.broadcasted_iota(jnp.int32, array.shape, 1)
    return jnp.sum(jnp.where(lanes == lane, array, 0.0), axis=1, keepdims=True)


def upright(row, offset, width):
    shape = (width, row.shape[1])
    lane = lax.broadcasted_iota(jnp.int32, shape, 1)
    at = lax.broadcasted_iota(jnp.int32, shape, 0) + offset
    return jnp.sum(jnp.where(lane == at, row, 0.0), axis=1, keepdims=True)


def flat(column):
    shape = (column.shape[0], BLOCK)
    diagonal = lax.broadcasted_iota(jnp.int32, shape, 0) == lax.broadcasted_iota(
        jnp.int32, shape, 1
    )
    return jnp.sum(jnp.where(diagonal, column, 0.0), axis=0, keepdims=True)


def causal_mask():
    shape = (BLOCK, BLOCK)
    row = lax.broadcasted_iota(jnp.int32, shape, 0)
    lane = lax.broadcasted_iota(jnp.int32, shape, 1)
    return jnp.where(lane >= row, 1.0, 0.0).astype(jnp.bfloat16)


def short_weights(taps_column, causal):
    high, low = split(rolled(flat(taps_column)))
    now = jnp.concatenate([high * causal, low * causal], axis=1)
    before = jnp.concatenate([high, low], axis=1) - now
    return jnp.concatenate([before, now], axis=0)


def short_filtered(window, m, rows, chosen, weights):
    def block_at(n):
        return window[m, rows, n * BLOCK : (n + 1) * BLOCK]

    now = jnp.concatenate([block_at(n) for n in chosen], axis=0)
    before = jnp.concatenate(
        [block_at(n - 1) if n else jnp.zeros_like(block_at(0)) for n in chosen], axis=0
    )
    both = jnp.concatenate([before, now], axis=1)
    return halves(jnp.dot(both, weights, preferred_element_type=jnp.float32))


def settle(source, target, held, fetched, kept):
    count = kept.shape[0]
    chunks = source.shape[0]
    height = source.shape[1] // count

    def fetch(i, chunk):
        rows = pl.ds(i * height, height)
        lanes = pl.ds(chunk * BLOCK, BLOCK)
        return pltpu.make_async_copy(
            source.at[chunk, rows, :], held.at[rows, lanes], fetched.at[i, chunk]
        )

    def keep(i):
        rows = pl.ds(i * height, height)
        return pltpu.make_async_copy(held.at[rows, :], target.at[rows, :], kept.at[i])

    for i in range(count):
        for chunk in range(chunks):
            fetch(i, chunk).start()
    for i in range(count):
        for chunk in range(chunks):
            fetch(i, chunk).wait()
        keep(i).start()
    for i in range(count):
        keep(i).wait()


def fused(
    total_channels,
    at_once,
    early_steps,
    streams,
    taps,
    pole_rates,
    residues_of,
    skips,
    gains,
    out,
    window,
    gated_at,
    filters,
    tables,
    held_at,
    squares,
    sums,
    scales,
    staged,
    early,
    early_staged,
    fetched,
    early_sent,
    early_got,
    early_kept,
    sums_sent,
    sums_got,
    block_sent,
    block_got,
    kept,
):
    chunks, owners, channels, _ = gated_at.shape
    width = pole_rates.shape[0]
    groups = channels // width
    steps = groups // at_once
    blocks = window.shape[2] // BLOCK
    across_count = lax.axis_size("ch")
    me = lax.axis_index("ctx")
    my_ch = lax.axis_index("ch")
    first_group = me * groups

    def fetch(step):
        rows = pl.ds(pl.multiple_of(step * (at_once * width), 16), at_once * width)
        return pltpu.make_async_copy(
            streams.at[:, rows, :], window.at[:, rows, :], fetched.at[step]
        )

    @pl.loop(0, steps)
    def _(step):
        fetch(step).start()

    def peer_ctx(by):
        return {"ctx": lax.rem(me + by, owners)}

    def peer(by):
        return {
            "ctx": lax.rem(me + lax.div(by, across_count), owners),
            "ch": lax.rem(my_ch + lax.rem(by, across_count), across_count),
        }

    devices = owners * across_count
    barrier = pltpu.get_barrier_semaphore()

    @pl.loop(1, devices)
    def _(by):
        pl.semaphore_signal(barrier, inc=1, device_id=peer(by), device_id_type=MESH)

    causal = causal_mask()

    def rows_of(group):
        return pl.ds(pl.multiple_of(group * width, 16), width)

    def per_channel(values, group):
        at = (first_group + group) * width
        return upright(values[pl.ds(lax.div(at, BLOCK), 1), :], lax.rem(at, BLOCK), width)

    def finish(group, chunk, held):
        chosen = range(chunk, blocks, chunks)
        value = short_filtered(window, 0, rows_of(group), chosen, filters[group])
        high, low, starts = (held[:, i * BLOCK : (i + 1) * BLOCK] for i in range(3))
        convolved = jnp.dot(
            jnp.concatenate([high, low, high, starts], axis=1),
            tables[group],
            preferred_element_type=jnp.float32,
        )
        skip = per_channel(skips, group)
        gain = per_channel(gains, group)
        shaped = (owners, width, BLOCK)
        product = (high.astype(jnp.float32) + low.astype(jnp.float32)).reshape(shaped)
        gated = value.reshape(shaped) * (convolved.reshape(shaped) + skip[None] * product)
        gated_at[chunk, :, rows_of(group), :] = gated * gain[None]
        return jnp.sum((gated * gated).reshape(owners, width // 8, 8, BLOCK), axis=1)

    def begin(group):
        at = first_group + group
        filters[group] = short_weights(picked(taps[0], at), causal)
        product = 1.0
        for m in (1, 2):
            product *= short_filtered(
                window, m, rows_of(group), range(blocks), short_weights(picked(taps[m], at), causal)
            )
        high, low = split(product)
        pair = jnp.concatenate([high, low], axis=1)

        rates = picked(pole_rates[...], at)
        residues = picked(residues_of[...], at)
        lags = lax.broadcasted_iota(jnp.int32, (width, BLOCK), 1).astype(jnp.float32)
        modes = residues * jnp.exp(-rates * lags)
        table_high, table_low = split(rolled(jnp.sum(modes, axis=0, keepdims=True)))
        table_high = table_high * causal
        lift_high, lift_low = split(residues * jnp.exp(-rates * (lags + 1.0)))
        spare = BLOCK - 3 * width
        tables[group] = jnp.concatenate(
            [
                table_high,
                table_high,
                table_low * causal,
                lift_high,
                lift_high,
                lift_low,
                jnp.zeros((spare, BLOCK), jnp.bfloat16),
            ],
            axis=0,
        )

        back_high, back_low = split(jnp.exp(-rates * (BLOCK - 1 - lags)))
        back = jnp.concatenate(
            [
                jnp.concatenate([back_high, back_high], axis=1),
                jnp.concatenate([back_low, back_low], axis=1),
            ],
            axis=0,
        )
        ends = lax.dot_general(
            back, pair, (((1,), (1,)), ((), ())), preferred_element_type=jnp.float32
        )
        states = ends[:width] + ends[width:]
        lane = lax.broadcasted_iota(jnp.int32, states.shape, 1)
        reach = 1
        while reach < blocks:
            earlier = pltpu.roll(states, reach * width, 1)
            decay = jnp.exp(-rates * (BLOCK * reach))
            states = states + jnp.where(lane >= reach * width, decay * earlier, 0.0)
            reach *= 2
        starts = jnp.where(lane >= width, pltpu.roll(states, width, 1), 0.0)
        starts_high, starts_low = (part.astype(jnp.float32) for part in split(starts))
        starts = jnp.concatenate(
            [
                starts_high,
                starts_low,
                starts_high,
                jnp.zeros((spare, starts.shape[1]), jnp.float32),
            ],
            axis=0,
        ).T.astype(jnp.bfloat16)
        held = jnp.concatenate([pair, starts], axis=1)

        def of_chunk(chunk):
            return jnp.concatenate(
                [held[n * width : (n + 1) * width] for n in range(chunk, blocks, chunks)], axis=0
            )

        for chunk in range(1, chunks):
            held_at[chunk - 1, group] = of_chunk(chunk)
        return of_chunk(0)

    early_channels = early_steps * at_once * width

    def early_copy(step, by):
        rows = pl.ds(pl.multiple_of(step * (at_once * width), 16), at_once * width)
        return pltpu.make_async_remote_copy(
            src_ref=gated_at.at[0, lax.rem(me + by, owners), rows, :],
            dst_ref=early.at[by, rows, :],
            send_sem=early_sent.at[step, by],
            recv_sem=early_got.at[step, by],
            device_id=peer_ctx(by),
            device_id_type=MESH,
        )

    def early_keep(by):
        source = lax.rem(me + owners - by, owners)
        return pltpu.make_async_copy(
            early_staged.at[by],
            out.at[0, pl.ds(pl.multiple_of(source * channels, 16), early_channels), :],
            early_kept.at[by],
        )

    def keep_early():
        @pl.loop(1, owners)
        def _(by):
            for step in range(early_steps):
                early_copy(step, by).wait()
            row = scales[0, pl.ds(me, 1), :]
            early_staged[by] = (early[by] * row).astype(jnp.bfloat16)
            early_keep(by).start()

    squares[...] = jnp.zeros_like(squares)

    @pl.loop(0, steps)
    def _(step):
        fetch(step).wait()
        begun = [begin(step * at_once + i) for i in range(at_once)]
        for i, held in enumerate(begun):
            squares[0] += finish(step * at_once + i, 0, held)

        if early_steps:

            @pl.when(step == 0)
            def _():
                pl.semaphore_wait(barrier, devices - 1)

            @pl.when(step < early_steps)
            def _():
                @pl.loop(1, owners)
                def _(by):
                    early_copy(step, by).start()

    def later(chunk, low, high):
        @pl.loop(low, high)
        def _(step):
            total = 0.0
            for i in range(at_once):
                group = step * at_once + i
                total += finish(group, chunk, held_at[chunk - 1, group])
            squares[chunk] += total

    def sums_copy(chunk, by):
        return pltpu.make_async_remote_copy(
            src_ref=sums.at[chunk, 0],
            dst_ref=sums.at[chunk, by],
            send_sem=sums_sent.at[chunk, by],
            recv_sem=sums_got.at[chunk, by],
            device_id=peer(by),
            device_id_type=MESH,
        )

    def place(chunk, owner, first):
        return out.at[
            chunk, pl.ds(pl.multiple_of(owner * channels + first, 16), channels - first), :
        ]

    def first_of(chunk):
        return early_channels if chunk == 0 else 0

    def block_copy(chunk, by, owner):
        first = first_of(chunk)
        return pltpu.make_async_remote_copy(
            src_ref=staged.at[chunk, by, first:, :],
            dst_ref=place(chunk, owner, first),
            send_sem=block_sent.at[chunk, by],
            recv_sem=block_got.at[chunk, by],
            device_id=peer_ctx(by),
            device_id_type=MESH,
        )

    def own_copy(chunk):
        return pltpu.make_async_copy(
            staged.at[chunk, 0], place(chunk, me, 0), kept.at[chunk]
        )

    def start_sums(chunk):
        sums[chunk, 0] = jnp.sum(squares[chunk], axis=1)

        @pl.loop(1, devices)
        def _(by):
            sums_copy(chunk, by).start()

    def start_blocks(chunk):
        @pl.loop(1, devices)
        def _(by):
            sums_copy(chunk, by).wait()

        total = jnp.sum(sums[chunk], axis=0)
        scales[chunk] = lax.rsqrt(total / total_channels + 1e-05)

        def fill(by, first):
            target = lax.rem(me + by, owners)
            row = scales[chunk, pl.ds(target, 1), :]
            staged[chunk, by, first:, :] = (gated_at[chunk, target, first:, :] * row).astype(
                jnp.bfloat16
            )

        @pl.loop(1, owners)
        def _(by):
            fill(by, first_of(chunk))
            block_copy(chunk, by, me).start()

        fill(0, 0)
        own_copy(chunk).start()

    def wait_blocks(chunk):
        own_copy(chunk).wait()

        @pl.loop(1, owners)
        def _(by):
            block_copy(chunk, by, me).wait_send()
            block_copy(chunk, by, lax.rem(me + owners - by, owners)).wait_recv()

    if not early_steps:
        pl.semaphore_wait(barrier, devices - 1)
    start_sums(0)
    for chunk in range(chunks):
        if chunk + 1 < chunks:
            later(chunk + 1, 0, steps)
            start_sums(chunk + 1)
        start_blocks(chunk)
    if early_steps:
        keep_early()
    for chunk in range(chunks):
        wait_blocks(chunk)
    if early_steps:

        @pl.loop(1, owners)
        def _(by):
            early_keep(by).wait()


def shards(total_channels, streams, short_taps, pole_rates, residues, skip, gain):
    owners = lax.axis_size("ctx")
    across = lax.axis_size("ch")
    channels, length = streams.shape[1:]
    groups = pole_rates.shape[0] // owners
    width = channels // groups
    assert pole_rates.shape[1] == width
    own = length // owners
    chunks = own // BLOCK
    later = max(chunks - 1, 1)
    devices = owners * across
    at_once = next(n for n in (2, 1) if groups % n == 0)
    steps = groups // at_once
    early_steps = steps // 2
    early_channels = max(early_steps, 1) * at_once * width
    vmem = pltpu.VMEM
    dma = pltpu.SemaphoreType.DMA
    f32 = jnp.float32
    bf16 = jnp.bfloat16
    moved = pl.pallas_call(
        functools.partial(fused, total_channels, at_once, early_steps),
        in_specs=[pl.BlockSpec(memory_space=pltpu.HBM)] + [pl.BlockSpec(memory_space=vmem)] * 5,
        out_specs=pl.BlockSpec(memory_space=pl.ANY),
        out_shape=jax.ShapeDtypeStruct((chunks, owners * channels, BLOCK), bf16),
        scratch_shapes=[
            vmem(streams.shape, bf16),
            vmem((chunks, owners, channels, BLOCK), f32),
            vmem((groups, 2 * BLOCK, 2 * BLOCK), bf16),
            vmem((groups, 4 * BLOCK, BLOCK), bf16),
            vmem((later, groups, owners * width, 3 * BLOCK), bf16),
            vmem((chunks, owners, 8, BLOCK), f32),
            vmem((chunks, devices, owners, BLOCK), f32),
            vmem((chunks, owners, BLOCK), f32),
            vmem((chunks, owners, channels, BLOCK), bf16),
            vmem((owners, early_channels, BLOCK), f32),
            vmem((owners, early_channels, BLOCK), bf16),
            dma((steps,)),
            dma((max(early_steps, 1), owners)),
            dma((max(early_steps, 1), owners)),
            dma((owners,)),
            dma((chunks, devices)),
            dma((chunks, devices)),
            dma((chunks, owners)),
            dma((chunks, owners)),
            dma((chunks,)),
        ],
        compiler_params=pltpu.CompilerParams(
            collective_id=0, has_side_effects=True, vmem_limit_bytes=56 * 1024 * 1024
        ),
    )(
        streams,
        short_taps.transpose(0, 2, 1),
        pole_rates.T,
        residues.T,
        skip.reshape(-1, BLOCK),
        gain.reshape(-1, BLOCK),
    )
    return pl.pallas_call(
        settle,
        in_specs=[pl.BlockSpec(memory_space=pl.ANY)],
        out_specs=pl.BlockSpec(memory_space=pl.ANY),
        out_shape=jax.ShapeDtypeStruct((owners * channels, own), bf16),
        scratch_shapes=[
            vmem((owners * channels, own), bf16),
            dma((4, chunks)),
            dma((4,)),
        ],
        compiler_params=pltpu.CompilerParams(vmem_limit_bytes=56 * 1024 * 1024),
    )(moved)


def solution(mesh):
    placed = (
        P(None, ("ch", "ctx"), None),
        P(None, "ch", None),
        P("ch", None),
        P("ch", None),
        P("ch"),
        P("ch"),
    )

    def whole(streams, *others):
        return jax.shard_map(
            functools.partial(shards, streams.shape[1]),
            mesh=mesh,
            in_specs=placed,
            out_specs=P("ch", "ctx"),
            check_vma=False,
        )(streams, *others)

    return whole
```

```python
import functools

import jax
import jax.numpy as jnp
from jax import lax
from jax.experimental import pallas as pl
from jax.experimental.pallas import tpu as pltpu
from jax.sharding import PartitionSpec as P

BLOCK = 128
MESH = pl.DeviceIdType.MESH


def split(value):
    high = value.astype(jnp.bfloat16)
    low = (value - high.astype(jnp.float32)).astype(jnp.bfloat16)
    return high, low


def halves(array):
    return array[:, :BLOCK] + array[:, BLOCK:]


def rolled(row):
    return pltpu.roll(
        jnp.broadcast_to(row, (BLOCK, BLOCK)), 0, 1, stride=1, stride_axis=0
    )


def picked(array, lane):
    lanes = lax.broadcasted_iota(jnp.int32, array.shape, 1)
    return jnp.sum(jnp.where(lanes == lane, array, 0.0), axis=1, keepdims=True)


def upright(row, offset, width):
    shape = (width, row.shape[1])
    lane = lax.broadcasted_iota(jnp.int32, shape, 1)
    at = lax.broadcasted_iota(jnp.int32, shape, 0) + offset
    return jnp.sum(jnp.where(lane == at, row, 0.0), axis=1, keepdims=True)


def flat(column):
    shape = (column.shape[0], BLOCK)
    diagonal = lax.broadcasted_iota(jnp.int32, shape, 0) == lax.broadcasted_iota(
        jnp.int32, shape, 1
    )
    return jnp.sum(jnp.where(diagonal, column, 0.0), axis=0, keepdims=True)


def causal_mask():
    shape = (BLOCK, BLOCK)
    row = lax.broadcasted_iota(jnp.int32, shape, 0)
    lane = lax.broadcasted_iota(jnp.int32, shape, 1)
    return jnp.where(lane >= row, 1.0, 0.0).astype(jnp.bfloat16)


def short_weights(taps_column, causal):
    high, low = split(rolled(flat(taps_column)))
    now = jnp.concatenate([high * causal, low * causal], axis=1)
    before = jnp.concatenate([high, low], axis=1) - now
    return jnp.concatenate([before, now], axis=0)


def short_filtered(window, m, rows, chosen, weights):
    def block_at(n):
        return window[m, rows, n * BLOCK : (n + 1) * BLOCK]

    now = jnp.concatenate([block_at(n) for n in chosen], axis=0)
    before = jnp.concatenate(
        [block_at(n - 1) if n else jnp.zeros_like(block_at(0)) for n in chosen], axis=0
    )
    both = jnp.concatenate([before, now], axis=1)
    return halves(jnp.dot(both, weights, preferred_element_type=jnp.float32))


def settle(source, target, held, fetched, kept):
    count = kept.shape[0]
    chunks = source.shape[0]
    height = source.shape[1] // count

    def fetch(i, chunk):
        rows = pl.ds(i * height, height)
        lanes = pl.ds(chunk * BLOCK, BLOCK)
        return pltpu.make_async_copy(
            source.at[chunk, rows, :], held.at[rows, lanes], fetched.at[i, chunk]
        )

    def keep(i):
        rows = pl.ds(i * height, height)
        return pltpu.make_async_copy(held.at[rows, :], target.at[rows, :], kept.at[i])

    for i in range(count):
        for chunk in range(chunks):
            fetch(i, chunk).start()
    for i in range(count):
        for chunk in range(chunks):
            fetch(i, chunk).wait()
        keep(i).start()
    for i in range(count):
        keep(i).wait()


def fused(
    total_channels,
    at_once,
    early_steps,
    streams,
    taps,
    pole_rates,
    residues_of,
    skips,
    gains,
    out,
    window,
    gated_at,
    filters,
    tables,
    backs,
    columns,
    states_at,
    held_at,
    squares,
    sums,
    scales,
    staged,
    early,
    early_staged,
    fetched,
    early_sent,
    early_got,
    early_kept,
    sums_sent,
    sums_got,
    block_sent,
    block_got,
    kept,
):
    chunks, owners, channels, _ = gated_at.shape
    width = pole_rates.shape[0]
    groups = channels // width
    steps = groups // at_once
    blocks = window.shape[2] // BLOCK
    across_count = lax.axis_size("ch")
    me = lax.axis_index("ctx")
    my_ch = lax.axis_index("ch")
    first_group = me * groups

    def fetch(step):
        rows = pl.ds(pl.multiple_of(step * (at_once * width), 16), at_once * width)
        return pltpu.make_async_copy(
            streams.at[:, rows, :], window.at[:, rows, :], fetched.at[step]
        )

    @pl.loop(0, steps)
    def _(step):
        fetch(step).start()

    def peer_ctx(by):
        return {"ctx": lax.rem(me + by, owners)}

    def peer(by):
        return {
            "ctx": lax.rem(me + lax.div(by, across_count), owners),
            "ch": lax.rem(my_ch + lax.rem(by, across_count), across_count),
        }

    devices = owners * across_count
    barrier = pltpu.get_barrier_semaphore()

    @pl.loop(1, devices)
    def _(by):
        pl.semaphore_signal(barrier, inc=1, device_id=peer(by), device_id_type=MESH)

    causal = causal_mask()

    def rows_of(group):
        return pl.ds(pl.multiple_of(group * width, 16), width)

    def per_channel(values, group):
        at = (first_group + group) * width
        return upright(values[pl.ds(lax.div(at, BLOCK), 1), :], lax.rem(at, BLOCK), width)

    def finish(group, chunk):
        chosen = range(chunk, blocks, chunks)
        value = short_filtered(window, 0, rows_of(group), chosen, filters[0, group])
        high, low, starts = (
            held_at[chunk, group, :, i * BLOCK : (i + 1) * BLOCK] for i in range(3)
        )
        convolved = jnp.dot(
            jnp.concatenate([high, low, high, starts], axis=1),
            tables[group],
            preferred_element_type=jnp.float32,
        )
        shaped = (owners, width, BLOCK)
        product = (high.astype(jnp.float32) + low.astype(jnp.float32)).reshape(shaped)
        gated = value.reshape(shaped) * (
            convolved.reshape(shaped) + columns[1, group][None] * product
        )
        gated_at[chunk, :, rows_of(group), :] = gated * columns[2, group][None]
        return jnp.sum((gated * gated).reshape(owners, width // 8, 8, BLOCK), axis=1)

    spare = BLOCK - 3 * width

    def tabulate(group):
        at = first_group + group
        for m in range(3):
            filters[m, group] = short_weights(picked(taps[m], at), causal)
        rates = jnp.broadcast_to(picked(pole_rates[...], at), (width, BLOCK))
        residues = picked(residues_of[...], at)
        columns[0, group] = rates
        columns[1, group] = jnp.broadcast_to(per_channel(skips, group), (width, BLOCK))
        columns[2, group] = jnp.broadcast_to(per_channel(gains, group), (width, BLOCK))
        lags = lax.broadcasted_iota(jnp.int32, (width, BLOCK), 1).astype(jnp.float32)
        modes = residues * jnp.exp(-rates * lags)
        table_high, table_low = split(rolled(jnp.sum(modes, axis=0, keepdims=True)))
        table_high = table_high * causal
        lift_high, lift_low = split(residues * jnp.exp(-rates * (lags + 1.0)))
        tables[group] = jnp.concatenate(
            [
                table_high,
                table_high,
                table_low * causal,
                lift_high,
                lift_high,
                lift_low,
                jnp.zeros((spare, BLOCK), jnp.bfloat16),
            ],
            axis=0,
        )
        back_high, back_low = split(jnp.exp(-rates * (BLOCK - 1 - lags)))
        backs[group] = jnp.concatenate(
            [
                jnp.concatenate([back_high, back_high], axis=1),
                jnp.concatenate([back_low, back_low], axis=1),
            ],
            axis=0,
        )

    def keep_held(group, array, lanes):
        for chunk in range(chunks):
            held_at[chunk, group, :, lanes] = jnp.concatenate(
                [array[n * width : (n + 1) * width] for n in range(chunk, blocks, chunks)], axis=0
            )

    def multiply(group):
        product = 1.0
        for m in (1, 2):
            product *= short_filtered(
                window, m, rows_of(group), range(blocks), filters[m, group]
            )
        high, low = split(product)
        pair = jnp.concatenate([high, low], axis=1)
        keep_held(group, pair, slice(0, 2 * BLOCK))
        ends = lax.dot_general(
            backs[group], pair, (((1,), (1,)), ((), ())), preferred_element_type=jnp.float32
        )
        states_at[group] = ends[:width] + ends[width:]

    def scan(some):
        shape = states_at.shape[1:]
        lane = lax.broadcasted_iota(jnp.int32, shape, 1)
        states = [states_at[group] for group in some]
        rates = [columns[0, group] for group in some]
        reach = 1
        while reach < blocks:
            earlier = [pltpu.roll(state, reach * width, 1) for state in states]
            decays = [jnp.exp(-rate * (BLOCK * reach)) for rate in rates]
            repeats = shape[1] // BLOCK
            states = [
                state
                + jnp.where(
                    lane >= reach * width, jnp.concatenate([decay] * repeats, axis=1) * before, 0.0
                )
                for state, decay, before in zip(states, decays, earlier)
            ]
            reach *= 2
        for group, state in zip(some, states):
            starts = jnp.where(lane >= width, pltpu.roll(state, width, 1), 0.0)
            starts_high, starts_low = (part.astype(jnp.float32) for part in split(starts))
            parts = [
                starts_high,
                starts_low,
                starts_high,
                jnp.zeros((spare, shape[1]), jnp.float32),
            ]
            upended = jnp.concatenate(parts, axis=0).T.astype(jnp.bfloat16)
            keep_held(group, upended, slice(2 * BLOCK, 3 * BLOCK))

    early_channels = early_steps * at_once * width

    def early_copy(step, by):
        rows = pl.ds(pl.multiple_of(step * (at_once * width), 16), at_once * width)
        return pltpu.make_async_remote_copy(
            src_ref=gated_at.at[0, lax.rem(me + by, owners), rows, :],
            dst_ref=early.at[by, rows, :],
            send_sem=early_sent.at[step, by],
            recv_sem=early_got.at[step, by],
            device_id=peer_ctx(by),
            device_id_type=MESH,
        )

    def early_keep(by):
        source = lax.rem(me + owners - by, owners)
        return pltpu.make_async_copy(
            early_staged.at[by],
            out.at[0, pl.ds(pl.multiple_of(source * channels, 16), early_channels), :],
            early_kept.at[by],
        )

    def keep_early():
        @pl.loop(1, owners)
        def _(by):
            for step in range(early_steps):
                early_copy(step, by).wait()
            row = scales[0, pl.ds(me, 1), :]
            early_staged[by] = (early[by] * row).astype(jnp.bfloat16)
            early_keep(by).start()

    squares[...] = jnp.zeros_like(squares)

    @pl.loop(0, steps)
    def _(step):
        for i in range(at_once):
            tabulate(step * at_once + i)

    @pl.loop(0, steps)
    def _(step):
        fetch(step).wait()
        for i in range(at_once):
            multiply(step * at_once + i)

    abreast = next(n for n in (8, 4, 2, 1) if groups % n == 0)

    @pl.loop(0, groups // abreast)
    def _(step):
        scan([step * abreast + i for i in range(abreast)])

    @pl.loop(0, steps)
    def _(step):
        squares[0] += sum(finish(step * at_once + i, 0) for i in range(at_once))

        if early_steps:

            @pl.when(step == 0)
            def _():
                pl.semaphore_wait(barrier, devices - 1)

            @pl.when(step < early_steps)
            def _():
                @pl.loop(1, owners)
                def _(by):
                    early_copy(step, by).start()

    def later(chunk, low, high):
        @pl.loop(low, high)
        def _(step):
            squares[chunk] += sum(finish(step * at_once + i, chunk) for i in range(at_once))

    def sums_copy(chunk, by):
        return pltpu.make_async_remote_copy(
            src_ref=sums.at[chunk, 0],
            dst_ref=sums.at[chunk, by],
            send_sem=sums_sent.at[chunk, by],
            recv_sem=sums_got.at[chunk, by],
            device_id=peer(by),
            device_id_type=MESH,
        )

    def place(chunk, owner, first):
        return out.at[
            chunk, pl.ds(pl.multiple_of(owner * channels + first, 16), channels - first), :
        ]

    def first_of(chunk):
        return early_channels if chunk == 0 else 0

    def block_copy(chunk, by, owner):
        first = first_of(chunk)
        return pltpu.make_async_remote_copy(
            src_ref=staged.at[chunk, by, first:, :],
            dst_ref=place(chunk, owner, first),
            send_sem=block_sent.at[chunk, by],
            recv_sem=block_got.at[chunk, by],
            device_id=peer_ctx(by),
            device_id_type=MESH,
        )

    def own_copy(chunk):
        return pltpu.make_async_copy(
            staged.at[chunk, 0], place(chunk, me, 0), kept.at[chunk]
        )

    def start_sums(chunk):
        sums[chunk, 0] = jnp.sum(squares[chunk], axis=1)

        @pl.loop(1, devices)
        def _(by):
            sums_copy(chunk, by).start()

    def start_blocks(chunk):
        @pl.loop(1, devices)
        def _(by):
            sums_copy(chunk, by).wait()

        total = jnp.sum(sums[chunk], axis=0)
        scales[chunk] = lax.rsqrt(total / total_channels + 1e-05)

        def fill(by, first):
            target = lax.rem(me + by, owners)
            row = scales[chunk, pl.ds(target, 1), :]
            staged[chunk, by, first:, :] = (gated_at[chunk, target, first:, :] * row).astype(
                jnp.bfloat16
            )

        @pl.loop(1, owners)
        def _(by):
            fill(by, first_of(chunk))
            block_copy(chunk, by, me).start()

        fill(0, 0)
        own_copy(chunk).start()

    def wait_blocks(chunk):
        own_copy(chunk).wait()

        @pl.loop(1, owners)
        def _(by):
            block_copy(chunk, by, me).wait_send()
            block_copy(chunk, by, lax.rem(me + owners - by, owners)).wait_recv()

    if not early_steps:
        pl.semaphore_wait(barrier, devices - 1)
    start_sums(0)
    for chunk in range(chunks):
        if chunk + 1 < chunks:
            later(chunk + 1, 0, steps)
            start_sums(chunk + 1)
        start_blocks(chunk)
    if early_steps:
        keep_early()
    for chunk in range(chunks):
        wait_blocks(chunk)
    if early_steps:

        @pl.loop(1, owners)
        def _(by):
            early_keep(by).wait()


def shards(total_channels, streams, short_taps, pole_rates, residues, skip, gain):
    owners = lax.axis_size("ctx")
    across = lax.axis_size("ch")
    channels, length = streams.shape[1:]
    groups = pole_rates.shape[0] // owners
    width = channels // groups
    assert pole_rates.shape[1] == width
    own = length // owners
    chunks = own // BLOCK
    devices = owners * across
    at_once = next(n for n in (4, 2, 1) if groups % n == 0)
    steps = groups // at_once
    early_steps = steps // 4
    early_channels = max(early_steps, 1) * at_once * width
    vmem = pltpu.VMEM
    dma = pltpu.SemaphoreType.DMA
    f32 = jnp.float32
    bf16 = jnp.bfloat16
    moved = pl.pallas_call(
        functools.partial(fused, total_channels, at_once, early_steps),
        in_specs=[pl.BlockSpec(memory_space=pltpu.HBM)] + [pl.BlockSpec(memory_space=vmem)] * 5,
        out_specs=pl.BlockSpec(memory_space=pl.ANY),
        out_shape=jax.ShapeDtypeStruct((chunks, owners * channels, BLOCK), bf16),
        scratch_shapes=[
            vmem(streams.shape, bf16),
            vmem((chunks, owners, channels, BLOCK), f32),
            vmem((3, groups, 2 * BLOCK, 2 * BLOCK), bf16),
            vmem((groups, 4 * BLOCK, BLOCK), bf16),
            vmem((groups, 2 * width, 2 * BLOCK), bf16),
            vmem((3, groups, width, BLOCK), f32),
            vmem((groups, width, length // BLOCK * width), f32),
            vmem((chunks, groups, owners * width, 3 * BLOCK), bf16),
            vmem((chunks, owners, 8, BLOCK), f32),
            vmem((chunks, devices, owners, BLOCK), f32),
            vmem((chunks, owners, BLOCK), f32),
            vmem((chunks, owners, channels, BLOCK), bf16),
            vmem((owners, early_channels, BLOCK), f32),
            vmem((owners, early_channels, BLOCK), bf16),
            dma((steps,)),
            dma((max(early_steps, 1), owners)),
            dma((max(early_steps, 1), owners)),
            dma((owners,)),
            dma((chunks, devices)),
            dma((chunks, devices)),
            dma((chunks, owners)),
            dma((chunks, owners)),
            dma((chunks,)),
        ],
        compiler_params=pltpu.CompilerParams(
            collective_id=0, has_side_effects=True, vmem_limit_bytes=56 * 1024 * 1024
        ),
    )(
        streams,
        short_taps.transpose(0, 2, 1),
        pole_rates.T,
        residues.T,
        skip.reshape(-1, BLOCK),
        gain.reshape(-1, BLOCK),
    )
    return pl.pallas_call(
        settle,
        in_specs=[pl.BlockSpec(memory_space=pl.ANY)],
        out_specs=pl.BlockSpec(memory_space=pl.ANY),
        out_shape=jax.ShapeDtypeStruct((owners * channels, own), bf16),
        scratch_shapes=[
            vmem((owners * channels, own), bf16),
            dma((4, chunks)),
            dma((4,)),
        ],
        compiler_params=pltpu.CompilerParams(vmem_limit_bytes=56 * 1024 * 1024),
    )(moved)


def solution(mesh):
    placed = (
        P(None, ("ch", "ctx"), None),
        P(None, "ch", None),
        P("ch", None),
        P("ch", None),
        P("ch"),
        P("ch"),
    )

    def whole(streams, *others):
        return jax.shard_map(
            functools.partial(shards, streams.shape[1]),
            mesh=mesh,
            in_specs=placed,
            out_specs=P("ch", "ctx"),
            check_vma=False,
        )(streams, *others)

    return whole
```

```python
import functools

import jax
import jax.numpy as jnp
from jax import lax
from jax.experimental import pallas as pl
from jax.experimental.pallas import tpu as pltpu
from jax.sharding import PartitionSpec as P

BLOCK = 128
MESH = pl.DeviceIdType.MESH


def split(value):
    high = value.astype(jnp.bfloat16)
    low = (value - high.astype(jnp.float32)).astype(jnp.bfloat16)
    return high, low


def halves(array):
    return array[:, :BLOCK] + array[:, BLOCK:]


def rolled(row):
    tile = pltpu.roll(jnp.broadcast_to(row, (8, BLOCK)), 0, 1, stride=1, stride_axis=0)
    return jnp.concatenate(
        [tile] + [pltpu.roll(tile, turn, 1) for turn in range(8, BLOCK, 8)], axis=0
    )


def picked(array, lane):
    lanes = lax.broadcasted_iota(jnp.int32, array.shape, 1)
    return jnp.sum(jnp.where(lanes == lane, array, 0.0), axis=1, keepdims=True)


def upright(row, offset, width):
    shape = (width, row.shape[1])
    lane = lax.broadcasted_iota(jnp.int32, shape, 1)
    at = lax.broadcasted_iota(jnp.int32, shape, 0) + offset
    return jnp.sum(jnp.where(lane == at, row, 0.0), axis=1, keepdims=True)


def flat(column):
    shape = (column.shape[0], BLOCK)
    diagonal = lax.broadcasted_iota(jnp.int32, shape, 0) == lax.broadcasted_iota(
        jnp.int32, shape, 1
    )
    return jnp.sum(jnp.where(diagonal, column, 0.0), axis=0, keepdims=True)


def causal_mask():
    shape = (BLOCK, BLOCK)
    row = lax.broadcasted_iota(jnp.int32, shape, 0)
    lane = lax.broadcasted_iota(jnp.int32, shape, 1)
    return jnp.where(lane >= row, 1.0, 0.0).astype(jnp.bfloat16)


def short_weights(taps_column, causal):
    high, low = split(rolled(flat(taps_column)))
    now = jnp.concatenate([high * causal, low * causal], axis=1)
    before = jnp.concatenate([high, low], axis=1) - now
    return jnp.concatenate([before, now], axis=0)


def short_filtered(window, m, rows, chosen, weights):
    def block_at(n):
        return window[m, rows, n * BLOCK : (n + 1) * BLOCK]

    now = jnp.concatenate([block_at(n) for n in chosen], axis=0)
    before = jnp.concatenate(
        [block_at(n - 1) if n else jnp.zeros_like(block_at(0)) for n in chosen], axis=0
    )
    both = jnp.concatenate([before, now], axis=1)
    return halves(jnp.dot(both, weights, preferred_element_type=jnp.float32))


def settle(source, target, held, fetched, kept):
    count = kept.shape[0]
    chunks = source.shape[0]
    height = source.shape[1] // count

    def fetch(i, chunk):
        rows = pl.ds(i * height, height)
        lanes = pl.ds(chunk * BLOCK, BLOCK)
        return pltpu.make_async_copy(
            source.at[chunk, rows, :], held.at[rows, lanes], fetched.at[i, chunk]
        )

    def keep(i):
        rows = pl.ds(i * height, height)
        return pltpu.make_async_copy(held.at[rows, :], target.at[rows, :], kept.at[i])

    for i in range(count):
        for chunk in range(chunks):
            fetch(i, chunk).start()
    for i in range(count):
        for chunk in range(chunks):
            fetch(i, chunk).wait()
        keep(i).start()
    for i in range(count):
        keep(i).wait()


def fused(
    total_channels,
    at_once,
    early_steps,
    streams,
    taps,
    pole_rates,
    residues_of,
    skips,
    gains,
    out,
    window,
    gated_at,
    filters,
    tables,
    held_at,
    squares,
    sums,
    scales,
    staged,
    early,
    early_staged,
    fetched,
    early_sent,
    early_got,
    early_kept,
    sums_sent,
    sums_got,
    block_sent,
    block_got,
    kept,
):
    chunks, owners, channels, _ = gated_at.shape
    width = pole_rates.shape[0]
    groups = channels // width
    steps = groups // at_once
    blocks = window.shape[2] // BLOCK
    across_count = lax.axis_size("ch")
    me = lax.axis_index("ctx")
    my_ch = lax.axis_index("ch")
    first_group = me * groups

    def fetch(step):
        rows = pl.ds(pl.multiple_of(step * (at_once * width), 16), at_once * width)
        return pltpu.make_async_copy(
            streams.at[:, rows, :], window.at[:, rows, :], fetched.at[step]
        )

    @pl.loop(0, steps)
    def _(step):
        fetch(step).start()

    def peer_ctx(by):
        return {"ctx": lax.rem(me + by, owners)}

    def peer(by):
        return {
            "ctx": lax.rem(me + lax.div(by, across_count), owners),
            "ch": lax.rem(my_ch + lax.rem(by, across_count), across_count),
        }

    devices = owners * across_count
    barrier = pltpu.get_barrier_semaphore()

    @pl.loop(1, devices)
    def _(by):
        pl.semaphore_signal(barrier, inc=1, device_id=peer(by), device_id_type=MESH)

    causal = causal_mask()

    def rows_of(group):
        return pl.ds(pl.multiple_of(group * width, 16), width)

    def per_channel(values, group):
        at = (first_group + group) * width
        return upright(values[pl.ds(lax.div(at, BLOCK), 1), :], lax.rem(at, BLOCK), width)

    def finish(group, chunk, held):
        chosen = range(chunk, blocks, chunks)
        value = short_filtered(window, 0, rows_of(group), chosen, filters[group])
        high, low, starts = (held[:, i * BLOCK : (i + 1) * BLOCK] for i in range(3))
        convolved = jnp.dot(
            jnp.concatenate([high, low, high, starts], axis=1),
            tables[group],
            preferred_element_type=jnp.float32,
        )
        skip = per_channel(skips, group)
        gain = per_channel(gains, group)
        shaped = (owners, width, BLOCK)
        product = (high.astype(jnp.float32) + low.astype(jnp.float32)).reshape(shaped)
        gated = value.reshape(shaped) * (convolved.reshape(shaped) + skip[None] * product)
        gated_at[chunk, :, rows_of(group), :] = gated * gain[None]
        return jnp.sum((gated * gated).reshape(owners, width // 8, 8, BLOCK), axis=1)

    def begin(group):
        at = first_group + group
        filters[group] = short_weights(picked(taps[0], at), causal)
        product = 1.0
        for m in (1, 2):
            product *= short_filtered(
                window, m, rows_of(group), range(blocks), short_weights(picked(taps[m], at), causal)
            )
        high, low = split(product)
        pair = jnp.concatenate([high, low], axis=1)

        rates = picked(pole_rates[...], at)
        residues = picked(residues_of[...], at)
        lags = lax.broadcasted_iota(jnp.int32, (width, BLOCK), 1).astype(jnp.float32)
        modes = residues * jnp.exp(-rates * lags)
        table_high, table_low = split(rolled(jnp.sum(modes, axis=0, keepdims=True)))
        table_high = table_high * causal
        lift_high, lift_low = split(residues * jnp.exp(-rates * (lags + 1.0)))
        spare = BLOCK - 3 * width
        tables[group] = jnp.concatenate(
            [
                table_high,
                table_high,
                table_low * causal,
                lift_high,
                lift_high,
                lift_low,
                jnp.zeros((spare, BLOCK), jnp.bfloat16),
            ],
            axis=0,
        )

        back_high, back_low = split(jnp.exp(-rates * (BLOCK - 1 - lags)))
        back = jnp.concatenate(
            [
                jnp.concatenate([back_high, back_high], axis=1),
                jnp.concatenate([back_low, back_low], axis=1),
            ],
            axis=0,
        )
        ends = lax.dot_general(
            back, pair, (((1,), (1,)), ((), ())), preferred_element_type=jnp.float32
        )
        states = ends[:width] + ends[width:]
        lane = lax.broadcasted_iota(jnp.int32, states.shape, 1)
        reach = 1
        while reach < blocks:
            earlier = pltpu.roll(states, reach * width, 1)
            decay = jnp.exp(-rates * (BLOCK * reach))
            states = states + jnp.where(lane >= reach * width, decay * earlier, 0.0)
            reach *= 2
        starts = jnp.where(lane >= width, pltpu.roll(states, width, 1), 0.0)
        starts_high, starts_low = (part.astype(jnp.float32) for part in split(starts))
        starts = jnp.concatenate(
            [
                starts_high,
                starts_low,
                starts_high,
                jnp.zeros((spare, starts.shape[1]), jnp.float32),
            ],
            axis=0,
        ).T.astype(jnp.bfloat16)
        held = jnp.concatenate([pair, starts], axis=1)

        def of_chunk(chunk):
            return jnp.concatenate(
                [held[n * width : (n + 1) * width] for n in range(chunk, blocks, chunks)], axis=0
            )

        for chunk in range(1, chunks):
            held_at[chunk - 1, group] = of_chunk(chunk)
        return of_chunk(0)

    early_channels = early_steps * at_once * width

    def early_copy(step, by):
        rows = pl.ds(pl.multiple_of(step * (at_once * width), 16), at_once * width)
        return pltpu.make_async_remote_copy(
            src_ref=gated_at.at[0, lax.rem(me + by, owners), rows, :],
            dst_ref=early.at[by, rows, :],
            send_sem=early_sent.at[step, by],
            recv_sem=early_got.at[step, by],
            device_id=peer_ctx(by),
            device_id_type=MESH,
        )

    def early_keep(by):
        source = lax.rem(me + owners - by, owners)
        return pltpu.make_async_copy(
            early_staged.at[by],
            out.at[0, pl.ds(pl.multiple_of(source * channels, 16), early_channels), :],
            early_kept.at[by],
        )

    def keep_early():
        @pl.loop(1, owners)
        def _(by):
            for step in range(early_steps):
                early_copy(step, by).wait()
            row = scales[0, pl.ds(me, 1), :]
            early_staged[by] = (early[by] * row).astype(jnp.bfloat16)
            early_keep(by).start()

    squares[...] = jnp.zeros_like(squares)

    @pl.loop(0, steps)
    def _(step):
        fetch(step).wait()
        begun = [begin(step * at_once + i) for i in range(at_once)]
        for i, held in enumerate(begun):
            squares[0] += finish(step * at_once + i, 0, held)

        if early_steps:

            @pl.when(step == 0)
            def _():
                pl.semaphore_wait(barrier, devices - 1)

            @pl.when(step < early_steps)
            def _():
                @pl.loop(1, owners)
                def _(by):
                    early_copy(step, by).start()

    def later(chunk, low, high):
        @pl.loop(low, high)
        def _(step):
            total = 0.0
            for i in range(at_once):
                group = step * at_once + i
                total += finish(group, chunk, held_at[chunk - 1, group])
            squares[chunk] += total

    def sums_copy(chunk, by):
        return pltpu.make_async_remote_copy(
            src_ref=sums.at[chunk, 0],
            dst_ref=sums.at[chunk, by],
            send_sem=sums_sent.at[chunk, by],
            recv_sem=sums_got.at[chunk, by],
            device_id=peer(by),
            device_id_type=MESH,
        )

    def place(chunk, owner, first):
        return out.at[
            chunk, pl.ds(pl.multiple_of(owner * channels + first, 16), channels - first), :
        ]

    def first_of(chunk):
        return early_channels if chunk == 0 else 0

    def block_copy(chunk, by, owner):
        first = first_of(chunk)
        return pltpu.make_async_remote_copy(
            src_ref=staged.at[chunk, by, first:, :],
            dst_ref=place(chunk, owner, first),
            send_sem=block_sent.at[chunk, by],
            recv_sem=block_got.at[chunk, by],
            device_id=peer_ctx(by),
            device_id_type=MESH,
        )

    def own_copy(chunk):
        return pltpu.make_async_copy(
            staged.at[chunk, 0], place(chunk, me, 0), kept.at[chunk]
        )

    def start_sums(chunk):
        sums[chunk, 0] = jnp.sum(squares[chunk], axis=1)

        @pl.loop(1, devices)
        def _(by):
            sums_copy(chunk, by).start()

    def start_blocks(chunk):
        @pl.loop(1, devices)
        def _(by):
            sums_copy(chunk, by).wait()

        total = jnp.sum(sums[chunk], axis=0)
        scales[chunk] = lax.rsqrt(total / total_channels + 1e-05)

        def fill(by, first):
            target = lax.rem(me + by, owners)
            row = scales[chunk, pl.ds(target, 1), :]
            staged[chunk, by, first:, :] = (gated_at[chunk, target, first:, :] * row).astype(
                jnp.bfloat16
            )

        @pl.loop(1, owners)
        def _(by):
            fill(by, first_of(chunk))
            block_copy(chunk, by, me).start()

        fill(0, 0)
        own_copy(chunk).start()

    def wait_blocks(chunk):
        own_copy(chunk).wait()

        @pl.loop(1, owners)
        def _(by):
            block_copy(chunk, by, me).wait_send()
            block_copy(chunk, by, lax.rem(me + owners - by, owners)).wait_recv()

    if not early_steps:
        pl.semaphore_wait(barrier, devices - 1)
    start_sums(0)
    for chunk in range(chunks):
        if chunk + 1 < chunks:
            later(chunk + 1, 0, steps)
            start_sums(chunk + 1)
        start_blocks(chunk)
    if early_steps:
        keep_early()
    for chunk in range(chunks):
        wait_blocks(chunk)
    if early_steps:

        @pl.loop(1, owners)
        def _(by):
            early_keep(by).wait()


def shards(total_channels, streams, short_taps, pole_rates, residues, skip, gain):
    owners = lax.axis_size("ctx")
    across = lax.axis_size("ch")
    channels, length = streams.shape[1:]
    groups = pole_rates.shape[0] // owners
    width = channels // groups
    assert pole_rates.shape[1] == width
    own = length // owners
    chunks = own // BLOCK
    later = max(chunks - 1, 1)
    devices = owners * across
    at_once = next(n for n in (2, 1) if groups % n == 0)
    steps = groups // at_once
    early_steps = steps // 2
    early_channels = max(early_steps, 1) * at_once * width
    vmem = pltpu.VMEM
    dma = pltpu.SemaphoreType.DMA
    f32 = jnp.float32
    bf16 = jnp.bfloat16
    moved = pl.pallas_call(
        functools.partial(fused, total_channels, at_once, early_steps),
        in_specs=[pl.BlockSpec(memory_space=pltpu.HBM)] + [pl.BlockSpec(memory_space=vmem)] * 5,
        out_specs=pl.BlockSpec(memory_space=pl.ANY),
        out_shape=jax.ShapeDtypeStruct((chunks, owners * channels, BLOCK), bf16),
        scratch_shapes=[
            vmem(streams.shape, bf16),
            vmem((chunks, owners, channels, BLOCK), f32),
            vmem((groups, 2 * BLOCK, 2 * BLOCK), bf16),
            vmem((groups, 4 * BLOCK, BLOCK), bf16),
            vmem((later, groups, owners * width, 3 * BLOCK), bf16),
            vmem((chunks, owners, 8, BLOCK), f32),
            vmem((chunks, devices, owners, BLOCK), f32),
            vmem((chunks, owners, BLOCK), f32),
            vmem((chunks, owners, channels, BLOCK), bf16),
            vmem((owners, early_channels, BLOCK), f32),
            vmem((owners, early_channels, BLOCK), bf16),
            dma((steps,)),
            dma((max(early_steps, 1), owners)),
            dma((max(early_steps, 1), owners)),
            dma((owners,)),
            dma((chunks, devices)),
            dma((chunks, devices)),
            dma((chunks, owners)),
            dma((chunks, owners)),
            dma((chunks,)),
        ],
        compiler_params=pltpu.CompilerParams(
            collective_id=0, has_side_effects=True, vmem_limit_bytes=56 * 1024 * 1024
        ),
    )(
        streams,
        short_taps.transpose(0, 2, 1),
        pole_rates.T,
        residues.T,
        skip.reshape(-1, BLOCK),
        gain.reshape(-1, BLOCK),
    )
    return pl.pallas_call(
        settle,
        in_specs=[pl.BlockSpec(memory_space=pl.ANY)],
        out_specs=pl.BlockSpec(memory_space=pl.ANY),
        out_shape=jax.ShapeDtypeStruct((owners * channels, own), bf16),
        scratch_shapes=[
            vmem((owners * channels, own), bf16),
            dma((4, chunks)),
            dma((4,)),
        ],
        compiler_params=pltpu.CompilerParams(vmem_limit_bytes=56 * 1024 * 1024),
    )(moved)


def solution(mesh):
    placed = (
        P(None, ("ch", "ctx"), None),
        P(None, "ch", None),
        P("ch", None),
        P("ch", None),
        P("ch"),
        P("ch"),
    )

    def whole(streams, *others):
        return jax.shard_map(
            functools.partial(shards, streams.shape[1]),
            mesh=mesh,
            in_specs=placed,
            out_specs=P("ch", "ctx"),
            check_vma=False,
        )(streams, *others)

    return whole
```

```python
import functools

import jax
import jax.numpy as jnp
from jax import lax
from jax.experimental import pallas as pl
from jax.experimental.pallas import tpu as pltpu
from jax.sharding import PartitionSpec as P

BLOCK = 128
MESH = pl.DeviceIdType.MESH


def split(value):
    high = value.astype(jnp.bfloat16)
    low = (value - high.astype(jnp.float32)).astype(jnp.bfloat16)
    return high, low


def halves(array):
    return array[:, :BLOCK] + array[:, BLOCK:]


def rolled(row):
    tile = pltpu.roll(jnp.broadcast_to(row, (8, BLOCK)), 0, 1, stride=1, stride_axis=0)
    return jnp.concatenate(
        [tile] + [pltpu.roll(tile, turn, 1) for turn in range(8, BLOCK, 8)], axis=0
    )


def picked(array, lane):
    lanes = lax.broadcasted_iota(jnp.int32, array.shape, 1)
    return jnp.sum(jnp.where(lanes == lane, array, 0.0), axis=1, keepdims=True)


def upright(row, offset, width):
    shape = (width, row.shape[1])
    lane = lax.broadcasted_iota(jnp.int32, shape, 1)
    at = lax.broadcasted_iota(jnp.int32, shape, 0) + offset
    return jnp.sum(jnp.where(lane == at, row, 0.0), axis=1, keepdims=True)


def flat(column):
    shape = (column.shape[0], BLOCK)
    diagonal = lax.broadcasted_iota(jnp.int32, shape, 0) == lax.broadcasted_iota(
        jnp.int32, shape, 1
    )
    return jnp.sum(jnp.where(diagonal, column, 0.0), axis=0, keepdims=True)


def causal_mask():
    shape = (BLOCK, BLOCK)
    row = lax.broadcasted_iota(jnp.int32, shape, 0)
    lane = lax.broadcasted_iota(jnp.int32, shape, 1)
    return jnp.where(lane >= row, 1.0, 0.0).astype(jnp.bfloat16)


def short_weights(taps_column, causal):
    high, low = split(rolled(flat(taps_column)))
    now = jnp.concatenate([high * causal, low * causal], axis=1)
    before = jnp.concatenate([high, low], axis=1) - now
    return jnp.concatenate([before, now], axis=0)


def short_filtered(window, m, rows, chosen, weights):
    def block_at(n):
        return window[m, rows, n * BLOCK : (n + 1) * BLOCK]

    now = jnp.concatenate([block_at(n) for n in chosen], axis=0)
    before = jnp.concatenate(
        [block_at(n - 1) if n else jnp.zeros_like(block_at(0)) for n in chosen], axis=0
    )
    both = jnp.concatenate([before, now], axis=1)
    return halves(jnp.dot(both, weights, preferred_element_type=jnp.float32))


def settle(source, target, held, fetched, kept):
    count = kept.shape[0]
    chunks = source.shape[0]
    height = source.shape[1] // count

    def fetch(i, chunk):
        rows = pl.ds(i * height, height)
        lanes = pl.ds(chunk * BLOCK, BLOCK)
        return pltpu.make_async_copy(
            source.at[chunk, rows, :], held.at[rows, lanes], fetched.at[i, chunk]
        )

    def keep(i):
        rows = pl.ds(i * height, height)
        return pltpu.make_async_copy(held.at[rows, :], target.at[rows, :], kept.at[i])

    for i in range(count):
        for chunk in range(chunks):
            fetch(i, chunk).start()
    for i in range(count):
        for chunk in range(chunks):
            fetch(i, chunk).wait()
        keep(i).start()
    for i in range(count):
        keep(i).wait()


def fused(
    total_channels,
    at_once,
    early_steps,
    streams,
    taps,
    pole_rates,
    residues_of,
    skips,
    gains,
    out,
    window,
    gated_at,
    filters,
    tables,
    held_at,
    squares,
    across,
    column,
    along,
    scales,
    staged,
    early,
    early_staged,
    fetched,
    early_sent,
    early_got,
    early_kept,
    across_sent,
    across_got,
    along_sent,
    along_got,
    block_sent,
    block_got,
    kept,
):
    chunks, owners, channels, _ = gated_at.shape
    width = pole_rates.shape[0]
    groups = channels // width
    steps = groups // at_once
    blocks = window.shape[2] // BLOCK
    across_count = lax.axis_size("ch")
    me = lax.axis_index("ctx")
    my_ch = lax.axis_index("ch")
    first_group = me * groups

    def fetch(step):
        rows = pl.ds(pl.multiple_of(step * (at_once * width), 16), at_once * width)
        return pltpu.make_async_copy(
            streams.at[:, rows, :], window.at[:, rows, :], fetched.at[step]
        )

    @pl.loop(0, steps)
    def _(step):
        fetch(step).start()

    def partner(by):
        result = 0
        bit = 1
        while bit < owners:
            mine, its = lax.rem(lax.div(me, bit), 2), lax.rem(lax.div(by, bit), 2)
            result = result + bit * (mine + its - 2 * mine * its)
            bit *= 2
        return result

    def far_first(i):
        return owners - i

    def peer_ctx(by):
        return {"ctx": partner(by)}

    def peer_ch(by):
        return {"ch": lax.rem(my_ch + by, across_count)}

    greeted = across_count + owners - 2
    barrier = pltpu.get_barrier_semaphore()

    @pl.loop(1, across_count)
    def _(by):
        pl.semaphore_signal(barrier, inc=1, device_id=peer_ch(by), device_id_type=MESH)

    @pl.loop(1, owners)
    def _(by):
        pl.semaphore_signal(barrier, inc=1, device_id=peer_ctx(by), device_id_type=MESH)

    causal = causal_mask()

    def rows_of(group):
        return pl.ds(pl.multiple_of(group * width, 16), width)

    def per_channel(values, group):
        at = (first_group + group) * width
        return upright(values[pl.ds(lax.div(at, BLOCK), 1), :], lax.rem(at, BLOCK), width)

    def finish(group, chunk, held):
        chosen = range(chunk, blocks, chunks)
        value = short_filtered(window, 0, rows_of(group), chosen, filters[group])
        high, low, starts = (held[:, i * BLOCK : (i + 1) * BLOCK] for i in range(3))
        convolved = jnp.dot(
            jnp.concatenate([high, low, high, starts], axis=1),
            tables[group],
            preferred_element_type=jnp.float32,
        )
        skip = per_channel(skips, group)
        gain = per_channel(gains, group)
        shaped = (owners, width, BLOCK)
        product = (high.astype(jnp.float32) + low.astype(jnp.float32)).reshape(shaped)
        gated = value.reshape(shaped) * (convolved.reshape(shaped) + skip[None] * product)
        gated_at[chunk, :, rows_of(group), :] = gated * gain[None]
        return jnp.sum((gated * gated).reshape(owners, width // 8, 8, BLOCK), axis=1)

    def begin(group):
        at = first_group + group
        filters[group] = short_weights(picked(taps[0], at), causal)
        product = 1.0
        for m in (1, 2):
            product *= short_filtered(
                window, m, rows_of(group), range(blocks), short_weights(picked(taps[m], at), causal)
            )
        high, low = split(product)
        pair = jnp.concatenate([high, low], axis=1)

        rates = picked(pole_rates[...], at)
        residues = picked(residues_of[...], at)
        lags = lax.broadcasted_iota(jnp.int32, (width, BLOCK), 1).astype(jnp.float32)
        modes = residues * jnp.exp(-rates * lags)
        table_high, table_low = split(rolled(jnp.sum(modes, axis=0, keepdims=True)))
        table_high = table_high * causal
        lift_high, lift_low = split(residues * jnp.exp(-rates * (lags + 1.0)))
        spare = BLOCK - 3 * width
        tables[group] = jnp.concatenate(
            [
                table_high,
                table_high,
                table_low * causal,
                lift_high,
                lift_high,
                lift_low,
                jnp.zeros((spare, BLOCK), jnp.bfloat16),
            ],
            axis=0,
        )

        back_high, back_low = split(jnp.exp(-rates * (BLOCK - 1 - lags)))
        back = jnp.concatenate(
            [
                jnp.concatenate([back_high, back_high], axis=1),
                jnp.concatenate([back_low, back_low], axis=1),
            ],
            axis=0,
        )
        ends = lax.dot_general(
            back, pair, (((1,), (1,)), ((), ())), preferred_element_type=jnp.float32
        )
        states = ends[:width] + ends[width:]
        lane = lax.broadcasted_iota(jnp.int32, states.shape, 1)
        reach = 1
        while reach < blocks:
            earlier = pltpu.roll(states, reach * width, 1)
            decay = jnp.exp(-rates * (BLOCK * reach))
            states = states + jnp.where(lane >= reach * width, decay * earlier, 0.0)
            reach *= 2
        starts = jnp.where(lane >= width, pltpu.roll(states, width, 1), 0.0)
        starts_high, starts_low = (part.astype(jnp.float32) for part in split(starts))
        starts = jnp.concatenate(
            [
                starts_high,
                starts_low,
                starts_high,
                jnp.zeros((spare, starts.shape[1]), jnp.float32),
            ],
            axis=0,
        ).T.astype(jnp.bfloat16)
        held = jnp.concatenate([pair, starts], axis=1)

        def of_chunk(chunk):
            return jnp.concatenate(
                [held[n * width : (n + 1) * width] for n in range(chunk, blocks, chunks)], axis=0
            )

        for chunk in range(1, chunks):
            held_at[chunk - 1, group] = of_chunk(chunk)
        return of_chunk(0)

    early_channels = early_steps * at_once * width

    def early_copy(step, by):
        rows = pl.ds(pl.multiple_of(step * (at_once * width), 16), at_once * width)
        return pltpu.make_async_remote_copy(
            src_ref=gated_at.at[0, partner(by), rows, :],
            dst_ref=early.at[by, rows, :],
            send_sem=early_sent.at[step, by],
            recv_sem=early_got.at[step, by],
            device_id=peer_ctx(by),
            device_id_type=MESH,
        )

    def early_keep(by):
        source = partner(by)
        return pltpu.make_async_copy(
            early_staged.at[by],
            out.at[0, pl.ds(pl.multiple_of(source * channels, 16), early_channels), :],
            early_kept.at[by],
        )

    def keep_early():
        @pl.loop(1, owners)
        def _(by):
            for step in range(early_steps):
                early_copy(step, by).wait()
            row = scales[0, pl.ds(me, 1), :]
            early_staged[by] = (early[by] * row).astype(jnp.bfloat16)
            early_keep(by).start()

    squares[...] = jnp.zeros_like(squares)

    @pl.loop(0, steps)
    def _(step):
        fetch(step).wait()
        begun = [begin(step * at_once + i) for i in range(at_once)]
        for i, held in enumerate(begun):
            squares[0] += finish(step * at_once + i, 0, held)

        if early_steps:

            @pl.when(step == 0)
            def _():
                pl.semaphore_wait(barrier, greeted)

            @pl.when(step < early_steps)
            def _():
                @pl.loop(1, owners)
                def _(i):
                    early_copy(step, far_first(i)).start()

    def later(chunk, low, high):
        @pl.loop(low, high)
        def _(step):
            total = 0.0
            for i in range(at_once):
                group = step * at_once + i
                total += finish(group, chunk, held_at[chunk - 1, group])
            squares[chunk] += total

    def across_copy(chunk, by):
        return pltpu.make_async_remote_copy(
            src_ref=across.at[chunk, 0],
            dst_ref=across.at[chunk, by],
            send_sem=across_sent.at[chunk, by],
            recv_sem=across_got.at[chunk, by],
            device_id=peer_ch(by),
            device_id_type=MESH,
        )

    def along_copy(chunk, by):
        return pltpu.make_async_remote_copy(
            src_ref=column.at[chunk],
            dst_ref=along.at[chunk, by],
            send_sem=along_sent.at[chunk, by],
            recv_sem=along_got.at[chunk, by],
            device_id=peer_ctx(by),
            device_id_type=MESH,
        )

    def place(chunk, owner, first):
        return out.at[
            chunk, pl.ds(pl.multiple_of(owner * channels + first, 16), channels - first), :
        ]

    def first_of(chunk):
        return early_channels if chunk == 0 else 0

    def block_copy(chunk, by, owner):
        first = first_of(chunk)
        return pltpu.make_async_remote_copy(
            src_ref=staged.at[chunk, by, first:, :],
            dst_ref=place(chunk, owner, first),
            send_sem=block_sent.at[chunk, by],
            recv_sem=block_got.at[chunk, by],
            device_id=peer_ctx(by),
            device_id_type=MESH,
        )

    def own_copy(chunk):
        return pltpu.make_async_copy(
            staged.at[chunk, 0], place(chunk, me, 0), kept.at[chunk]
        )

    def start_across(chunk):
        across[chunk, 0] = jnp.sum(squares[chunk], axis=1)

        @pl.loop(1, across_count)
        def _(by):
            across_copy(chunk, by).start()

    def start_along(chunk):
        @pl.loop(1, across_count)
        def _(by):
            across_copy(chunk, by).wait()

        column[chunk] = jnp.sum(across[chunk], axis=0)

        @pl.loop(1, owners)
        def _(i):
            along_copy(chunk, far_first(i)).start()

    def fill_blocks(chunk):
        along[chunk, 0] = column[chunk]

        @pl.loop(1, owners)
        def _(by):
            along_copy(chunk, by).wait()

        total = jnp.sum(along[chunk], axis=0)
        scales[chunk] = lax.rsqrt(total / total_channels + 1e-05)

        def fill(by, first):
            target = partner(by)
            row = scales[chunk, pl.ds(target, 1), :]
            staged[chunk, by, first:, :] = (gated_at[chunk, target, first:, :] * row).astype(
                jnp.bfloat16
            )

        @pl.loop(1, owners)
        def _(by):
            fill(by, first_of(chunk))

        fill(0, 0)
        own_copy(chunk).start()

    def start_blocks(chunk):
        @pl.loop(1, owners)
        def _(i):
            block_copy(chunk, far_first(i), me).start()

    def wait_blocks(chunk):
        own_copy(chunk).wait()

        @pl.loop(1, owners)
        def _(by):
            block_copy(chunk, by, me).wait_send()
            block_copy(chunk, by, partner(by)).wait_recv()

    if not early_steps:
        pl.semaphore_wait(barrier, greeted)
    start_across(0)
    for chunk in range(chunks):
        more = chunk + 1 < chunks
        if more and chunk == 0:
            later(1, 0, steps // 2)
        if chunk == 0:
            start_along(0)
        if more:
            later(chunk + 1, steps // 2 if chunk == 0 else 0, steps)
            start_across(chunk + 1)
        fill_blocks(chunk)
        if more:
            start_along(chunk + 1)
        start_blocks(chunk)
    if early_steps:
        keep_early()
    for chunk in range(chunks):
        wait_blocks(chunk)
    if early_steps:

        @pl.loop(1, owners)
        def _(by):
            early_keep(by).wait()


def shards(total_channels, streams, short_taps, pole_rates, residues, skip, gain):
    owners = lax.axis_size("ctx")
    across = lax.axis_size("ch")
    channels, length = streams.shape[1:]
    groups = pole_rates.shape[0] // owners
    width = channels // groups
    assert pole_rates.shape[1] == width
    own = length // owners
    chunks = own // BLOCK
    later = max(chunks - 1, 1)
    at_once = next(n for n in (2, 1) if groups % n == 0)
    steps = groups // at_once
    early_steps = steps // 2
    early_channels = max(early_steps, 1) * at_once * width
    vmem = pltpu.VMEM
    dma = pltpu.SemaphoreType.DMA
    f32 = jnp.float32
    bf16 = jnp.bfloat16
    moved = pl.pallas_call(
        functools.partial(fused, total_channels, at_once, early_steps),
        in_specs=[pl.BlockSpec(memory_space=pltpu.HBM)] + [pl.BlockSpec(memory_space=vmem)] * 5,
        out_specs=pl.BlockSpec(memory_space=pl.ANY),
        out_shape=jax.ShapeDtypeStruct((chunks, owners * channels, BLOCK), bf16),
        scratch_shapes=[
            vmem(streams.shape, bf16),
            vmem((chunks, owners, channels, BLOCK), f32),
            vmem((groups, 2 * BLOCK, 2 * BLOCK), bf16),
            vmem((groups, 4 * BLOCK, BLOCK), bf16),
            vmem((later, groups, owners * width, 3 * BLOCK), bf16),
            vmem((chunks, owners, 8, BLOCK), f32),
            vmem((chunks, across, owners, BLOCK), f32),
            vmem((chunks, owners, BLOCK), f32),
            vmem((chunks, owners, owners, BLOCK), f32),
            vmem((chunks, owners, BLOCK), f32),
            vmem((chunks, owners, channels, BLOCK), bf16),
            vmem((owners, early_channels, BLOCK), f32),
            vmem((owners, early_channels, BLOCK), bf16),
            dma((steps,)),
            dma((max(early_steps, 1), owners)),
            dma((max(early_steps, 1), owners)),
            dma((owners,)),
            dma((chunks, across)),
            dma((chunks, across)),
            dma((chunks, owners)),
            dma((chunks, owners)),
            dma((chunks, owners)),
            dma((chunks, owners)),
            dma((chunks,)),
        ],
        compiler_params=pltpu.CompilerParams(
            collective_id=0, has_side_effects=True, vmem_limit_bytes=56 * 1024 * 1024
        ),
    )(
        streams,
        short_taps.transpose(0, 2, 1),
        pole_rates.T,
        residues.T,
        skip.reshape(-1, BLOCK),
        gain.reshape(-1, BLOCK),
    )
    return pl.pallas_call(
        settle,
        in_specs=[pl.BlockSpec(memory_space=pl.ANY)],
        out_specs=pl.BlockSpec(memory_space=pl.ANY),
        out_shape=jax.ShapeDtypeStruct((owners * channels, own), bf16),
        scratch_shapes=[
            vmem((owners * channels, own), bf16),
            dma((4, chunks)),
            dma((4,)),
        ],
        compiler_params=pltpu.CompilerParams(vmem_limit_bytes=56 * 1024 * 1024),
    )(moved)


def solution(mesh):
    placed = (
        P(None, ("ch", "ctx"), None),
        P(None, "ch", None),
        P("ch", None),
        P("ch", None),
        P("ch"),
        P("ch"),
    )

    def whole(streams, *others):
        return jax.shard_map(
            functools.partial(shards, streams.shape[1]),
            mesh=mesh,
            in_specs=placed,
            out_specs=P("ch", "ctx"),
            check_vma=False,
        )(streams, *others)

    return whole
```

```python
import functools

import jax
import jax.numpy as jnp
from jax import lax
from jax.experimental import pallas as pl
from jax.experimental.pallas import tpu as pltpu
from jax.sharding import PartitionSpec as P

BLOCK = 128
MESH = pl.DeviceIdType.MESH


def split(value):
    high = value.astype(jnp.bfloat16)
    low = (value - high.astype(jnp.float32)).astype(jnp.bfloat16)
    return high, low


def halves(array):
    return array[:, :BLOCK] + array[:, BLOCK:]


def rolled(row):
    tile = pltpu.roll(jnp.broadcast_to(row, (8, BLOCK)), 0, 1, stride=1, stride_axis=0)
    return jnp.concatenate(
        [tile] + [pltpu.roll(tile, turn, 1) for turn in range(8, BLOCK, 8)], axis=0
    )


def picked(array, lane):
    lanes = lax.broadcasted_iota(jnp.int32, array.shape, 1)
    return jnp.sum(jnp.where(lanes == lane, array, 0.0), axis=1, keepdims=True)


def upright(row, offset, width):
    shape = (width, row.shape[1])
    lane = lax.broadcasted_iota(jnp.int32, shape, 1)
    at = lax.broadcasted_iota(jnp.int32, shape, 0) + offset
    return jnp.sum(jnp.where(lane == at, row, 0.0), axis=1, keepdims=True)


def flat(column):
    shape = (column.shape[0], BLOCK)
    diagonal = lax.broadcasted_iota(jnp.int32, shape, 0) == lax.broadcasted_iota(
        jnp.int32, shape, 1
    )
    return jnp.sum(jnp.where(diagonal, column, 0.0), axis=0, keepdims=True)


def causal_mask():
    shape = (BLOCK, BLOCK)
    row = lax.broadcasted_iota(jnp.int32, shape, 0)
    lane = lax.broadcasted_iota(jnp.int32, shape, 1)
    return jnp.where(lane >= row, 1.0, 0.0).astype(jnp.bfloat16)


def short_weights(taps_column, causal):
    high, low = split(rolled(flat(taps_column)))
    now = jnp.concatenate([high * causal, low * causal], axis=1)
    before = jnp.concatenate([high, low], axis=1) - now
    return jnp.concatenate([before, now], axis=0)


def short_filtered(window, m, rows, chosen, weights):
    def block_at(n):
        return window[m, rows, n * BLOCK : (n + 1) * BLOCK]

    now = jnp.concatenate([block_at(n) for n in chosen], axis=0)
    before = jnp.concatenate(
        [block_at(n - 1) if n else jnp.zeros_like(block_at(0)) for n in chosen], axis=0
    )
    both = jnp.concatenate([before, now], axis=1)
    return halves(jnp.dot(both, weights, preferred_element_type=jnp.float32))


def settle(source, target, held, fetched, kept):
    count = kept.shape[0]
    chunks = source.shape[0]
    height = source.shape[1] // count

    def fetch(i, chunk):
        rows = pl.ds(i * height, height)
        lanes = pl.ds(chunk * BLOCK, BLOCK)
        return pltpu.make_async_copy(
            source.at[chunk, rows, :], held.at[rows, lanes], fetched.at[i, chunk]
        )

    def keep(i):
        rows = pl.ds(i * height, height)
        return pltpu.make_async_copy(held.at[rows, :], target.at[rows, :], kept.at[i])

    for i in range(count):
        for chunk in range(chunks):
            fetch(i, chunk).start()
    for i in range(count):
        for chunk in range(chunks):
            fetch(i, chunk).wait()
        keep(i).start()
    for i in range(count):
        keep(i).wait()


def fused(
    total_channels,
    at_once,
    early_steps,
    streams,
    taps,
    pole_rates,
    residues_of,
    skips,
    gains,
    out,
    window,
    gated_at,
    filters,
    tables,
    held_at,
    squares,
    across,
    column,
    along,
    scales,
    staged,
    early,
    early_staged,
    fetched,
    early_sent,
    early_got,
    early_kept,
    across_sent,
    across_got,
    along_sent,
    along_got,
    block_sent,
    block_got,
    kept,
):
    chunks, owners, channels, _ = gated_at.shape
    width = pole_rates.shape[0]
    groups = channels // width
    steps = groups // at_once
    blocks = window.shape[2] // BLOCK
    across_count = lax.axis_size("ch")
    me = lax.axis_index("ctx")
    my_ch = lax.axis_index("ch")
    first_group = me * groups

    def fetch(step):
        rows = pl.ds(pl.multiple_of(step * (at_once * width), 16), at_once * width)
        return pltpu.make_async_copy(
            streams.at[:, rows, :], window.at[:, rows, :], fetched.at[step]
        )

    @pl.loop(0, steps)
    def _(step):
        fetch(step).start()

    def partner(by):
        result = 0
        bit = 1
        while bit < owners:
            mine, its = lax.rem(lax.div(me, bit), 2), lax.rem(lax.div(by, bit), 2)
            result = result + bit * (mine + its - 2 * mine * its)
            bit *= 2
        return result

    def far_first(i):
        return owners - i

    def peer_ctx(by):
        return {"ctx": partner(by)}

    def peer_ch(by):
        return {"ch": lax.rem(my_ch + by, across_count)}

    greeted = across_count + owners - 2
    barrier = pltpu.get_barrier_semaphore()

    @pl.loop(1, across_count)
    def _(by):
        pl.semaphore_signal(barrier, inc=1, device_id=peer_ch(by), device_id_type=MESH)

    @pl.loop(1, owners)
    def _(by):
        pl.semaphore_signal(barrier, inc=1, device_id=peer_ctx(by), device_id_type=MESH)

    causal = causal_mask()

    def rows_of(group):
        return pl.ds(pl.multiple_of(group * width, 16), width)

    def per_channel(values, group):
        at = (first_group + group) * width
        return upright(values[pl.ds(lax.div(at, BLOCK), 1), :], lax.rem(at, BLOCK), width)

    def finish(group, chunk, held):
        chosen = range(chunk, blocks, chunks)
        value = short_filtered(window, 0, rows_of(group), chosen, filters[group])
        high, low, starts = (held[:, i * BLOCK : (i + 1) * BLOCK] for i in range(3))
        convolved = jnp.dot(
            jnp.concatenate([high, low, high, starts], axis=1),
            tables[group],
            preferred_element_type=jnp.float32,
        )
        skip = per_channel(skips, group)
        gain = per_channel(gains, group)
        shaped = (owners, width, BLOCK)
        product = (high.astype(jnp.float32) + low.astype(jnp.float32)).reshape(shaped)
        gated = value.reshape(shaped) * (convolved.reshape(shaped) + skip[None] * product)
        gated_at[chunk, :, rows_of(group), :] = gated * gain[None]
        return jnp.sum((gated * gated).reshape(owners, width // 8, 8, BLOCK), axis=1)

    def begin(group):
        at = first_group + group
        filters[group] = short_weights(picked(taps[0], at), causal)
        product = 1.0
        for m in (1, 2):
            product *= short_filtered(
                window, m, rows_of(group), range(blocks), short_weights(picked(taps[m], at), causal)
            )
        high, low = split(product)
        pair = jnp.concatenate([high, low], axis=1)

        rates = picked(pole_rates[...], at)
        residues = picked(residues_of[...], at)
        lags = lax.broadcasted_iota(jnp.int32, (width, BLOCK), 1).astype(jnp.float32)
        modes = residues * jnp.exp(-rates * lags)
        table_high, table_low = split(rolled(jnp.sum(modes, axis=0, keepdims=True)))
        table_high = table_high * causal
        lift_high, lift_low = split(residues * jnp.exp(-rates * (lags + 1.0)))
        spare = BLOCK - 3 * width
        tables[group] = jnp.concatenate(
            [
                table_high,
                table_high,
                table_low * causal,
                lift_high,
                lift_high,
                lift_low,
                jnp.zeros((spare, BLOCK), jnp.bfloat16),
            ],
            axis=0,
        )

        back_high, back_low = split(jnp.exp(-rates * (BLOCK - 1 - lags)))
        back = jnp.concatenate(
            [
                jnp.concatenate([back_high, back_high], axis=1),
                jnp.concatenate([back_low, back_low], axis=1),
            ],
            axis=0,
        )
        ends = lax.dot_general(
            back, pair, (((1,), (1,)), ((), ())), preferred_element_type=jnp.float32
        )
        states = ends[:width] + ends[width:]
        lane = lax.broadcasted_iota(jnp.int32, states.shape, 1)
        reach = 1
        while reach < blocks:
            earlier = pltpu.roll(states, reach * width, 1)
            decay = jnp.exp(-rates * (BLOCK * reach))
            states = states + jnp.where(lane >= reach * width, decay * earlier, 0.0)
            reach *= 2
        starts = jnp.where(lane >= width, pltpu.roll(states, width, 1), 0.0)
        starts_high, starts_low = (part.astype(jnp.float32) for part in split(starts))
        starts = jnp.concatenate(
            [
                starts_high,
                starts_low,
                starts_high,
                jnp.zeros((spare, starts.shape[1]), jnp.float32),
            ],
            axis=0,
        ).T.astype(jnp.bfloat16)
        held = jnp.concatenate([pair, starts], axis=1)

        def of_chunk(chunk):
            return jnp.concatenate(
                [held[n * width : (n + 1) * width] for n in range(chunk, blocks, chunks)], axis=0
            )

        for chunk in range(1, chunks):
            held_at[chunk - 1, group] = of_chunk(chunk)
        return of_chunk(0)

    early_channels = early_steps * at_once * width

    def early_copy(step, by):
        rows = pl.ds(pl.multiple_of(step * (at_once * width), 16), at_once * width)
        return pltpu.make_async_remote_copy(
            src_ref=gated_at.at[0, partner(by), rows, :],
            dst_ref=early.at[by, rows, :],
            send_sem=early_sent.at[step, by],
            recv_sem=early_got.at[step, by],
            device_id=peer_ctx(by),
            device_id_type=MESH,
        )

    def early_keep(by):
        source = partner(by)
        return pltpu.make_async_copy(
            early_staged.at[by],
            out.at[0, pl.ds(pl.multiple_of(source * channels, 16), early_channels), :],
            early_kept.at[by],
        )

    def keep_early():
        @pl.loop(1, owners)
        def _(by):
            for step in range(early_steps):
                early_copy(step, by).wait()
            row = scales[0, pl.ds(me, 1), :]
            early_staged[by] = (early[by] * row).astype(jnp.bfloat16)
            early_keep(by).start()

    squares[...] = jnp.zeros_like(squares)

    @pl.loop(0, steps)
    def _(step):
        fetch(step).wait()
        begun = [begin(step * at_once + i) for i in range(at_once)]
        for i, held in enumerate(begun):
            squares[0] += finish(step * at_once + i, 0, held)

        if early_steps:

            @pl.when(step == 0)
            def _():
                pl.semaphore_wait(barrier, greeted)

            @pl.when(step < early_steps)
            def _():
                @pl.loop(1, owners)
                def _(i):
                    early_copy(step, far_first(i)).start()

    def later(chunk, low, high):
        @pl.loop(low, high)
        def _(step):
            total = 0.0
            for i in range(at_once):
                group = step * at_once + i
                total += finish(group, chunk, held_at[chunk - 1, group])
            squares[chunk] += total

    def across_copy(chunk, by):
        return pltpu.make_async_remote_copy(
            src_ref=across.at[chunk, 0],
            dst_ref=across.at[chunk, by],
            send_sem=across_sent.at[chunk, by],
            recv_sem=across_got.at[chunk, by],
            device_id=peer_ch(by),
            device_id_type=MESH,
        )

    def along_copy(chunk, by):
        return pltpu.make_async_remote_copy(
            src_ref=column.at[chunk],
            dst_ref=along.at[chunk, by],
            send_sem=along_sent.at[chunk, by],
            recv_sem=along_got.at[chunk, by],
            device_id=peer_ctx(by),
            device_id_type=MESH,
        )

    def place(chunk, owner, first):
        return out.at[
            chunk, pl.ds(pl.multiple_of(owner * channels + first, 16), channels - first), :
        ]

    def first_of(chunk):
        return early_channels if chunk == 0 else 0

    def block_copy(chunk, by, owner):
        first = first_of(chunk)
        return pltpu.make_async_remote_copy(
            src_ref=staged.at[chunk, by, first:, :],
            dst_ref=place(chunk, owner, first),
            send_sem=block_sent.at[chunk, by],
            recv_sem=block_got.at[chunk, by],
            device_id=peer_ctx(by),
            device_id_type=MESH,
        )

    def own_copy(chunk):
        return pltpu.make_async_copy(
            staged.at[chunk, 0], place(chunk, me, 0), kept.at[chunk]
        )

    def start_across(chunk):
        across[chunk, 0] = jnp.sum(squares[chunk], axis=1)

        @pl.loop(1, across_count)
        def _(by):
            across_copy(chunk, by).start()

    def start_along(chunk):
        @pl.loop(1, across_count)
        def _(by):
            across_copy(chunk, by).wait()

        column[chunk] = jnp.sum(across[chunk], axis=0)

        @pl.loop(1, owners)
        def _(i):
            along_copy(chunk, far_first(i)).start()

    def send_blocks(chunk, meanwhile):
        along[chunk, 0] = column[chunk]

        @pl.loop(1, owners)
        def _(by):
            along_copy(chunk, by).wait()

        total = jnp.sum(along[chunk], axis=0)
        scales[chunk] = lax.rsqrt(total / total_channels + 1e-05)

        def fill(by, first):
            target = partner(by)
            row = scales[chunk, pl.ds(target, 1), :]
            staged[chunk, by, first:, :] = (gated_at[chunk, target, first:, :] * row).astype(
                jnp.bfloat16
            )

        def send(i):
            by = far_first(i)
            fill(by, first_of(chunk))
            block_copy(chunk, by, me).start()

        cut = min(4, owners)
        pl.loop(1, cut)(send)
        meanwhile()
        pl.loop(cut, owners)(send)
        fill(0, 0)
        own_copy(chunk).start()

    def wait_blocks(chunk):
        own_copy(chunk).wait()

        @pl.loop(1, owners)
        def _(by):
            block_copy(chunk, by, me).wait_send()
            block_copy(chunk, by, partner(by)).wait_recv()

    if not early_steps:
        pl.semaphore_wait(barrier, greeted)
    start_across(0)
    for chunk in range(chunks):
        more = chunk + 1 < chunks
        if more and chunk == 0:
            later(1, 0, steps // 2)
        if chunk == 0:
            start_along(0)
        if more:
            later(chunk + 1, steps // 2 if chunk == 0 else 0, steps)
            start_across(chunk + 1)
        send_blocks(chunk, functools.partial(start_along, chunk + 1) if more else lambda: None)
    if early_steps:
        keep_early()
    for chunk in range(chunks):
        wait_blocks(chunk)
    if early_steps:

        @pl.loop(1, owners)
        def _(by):
            early_keep(by).wait()


def shards(total_channels, streams, short_taps, pole_rates, residues, skip, gain):
    owners = lax.axis_size("ctx")
    across = lax.axis_size("ch")
    channels, length = streams.shape[1:]
    groups = pole_rates.shape[0] // owners
    width = channels // groups
    assert pole_rates.shape[1] == width
    own = length // owners
    assert owners & (owners - 1) == 0
    chunks = own // BLOCK
    later = max(chunks - 1, 1)
    at_once = next(n for n in (2, 1) if groups % n == 0)
    steps = groups // at_once
    early_steps = 3 * steps // 8
    early_channels = max(early_steps, 1) * at_once * width
    vmem = pltpu.VMEM
    dma = pltpu.SemaphoreType.DMA
    f32 = jnp.float32
    bf16 = jnp.bfloat16
    moved = pl.pallas_call(
        functools.partial(fused, total_channels, at_once, early_steps),
        in_specs=[pl.BlockSpec(memory_space=pltpu.HBM)] + [pl.BlockSpec(memory_space=vmem)] * 5,
        out_specs=pl.BlockSpec(memory_space=pl.ANY),
        out_shape=jax.ShapeDtypeStruct((chunks, owners * channels, BLOCK), bf16),
        scratch_shapes=[
            vmem(streams.shape, bf16),
            vmem((chunks, owners, channels, BLOCK), f32),
            vmem((groups, 2 * BLOCK, 2 * BLOCK), bf16),
            vmem((groups, 4 * BLOCK, BLOCK), bf16),
            vmem((later, groups, owners * width, 3 * BLOCK), bf16),
            vmem((chunks, owners, 8, BLOCK), f32),
            vmem((chunks, across, owners, BLOCK), f32),
            vmem((chunks, owners, BLOCK), f32),
            vmem((chunks, owners, owners, BLOCK), f32),
            vmem((chunks, owners, BLOCK), f32),
            vmem((chunks, owners, channels, BLOCK), bf16),
            vmem((owners, early_channels, BLOCK), f32),
            vmem((owners, early_channels, BLOCK), bf16),
            dma((steps,)),
            dma((max(early_steps, 1), owners)),
            dma((max(early_steps, 1), owners)),
            dma((owners,)),
            dma((chunks, across)),
            dma((chunks, across)),
            dma((chunks, owners)),
            dma((chunks, owners)),
            dma((chunks, owners)),
            dma((chunks, owners)),
            dma((chunks,)),
        ],
        compiler_params=pltpu.CompilerParams(
            collective_id=0, has_side_effects=True, vmem_limit_bytes=56 * 1024 * 1024
        ),
    )(
        streams,
        short_taps.transpose(0, 2, 1),
        pole_rates.T,
        residues.T,
        skip.reshape(-1, BLOCK),
        gain.reshape(-1, BLOCK),
    )
    return pl.pallas_call(
        settle,
        in_specs=[pl.BlockSpec(memory_space=pl.ANY)],
        out_specs=pl.BlockSpec(memory_space=pl.ANY),
        out_shape=jax.ShapeDtypeStruct((owners * channels, own), bf16),
        scratch_shapes=[
            vmem((owners * channels, own), bf16),
            dma((4, chunks)),
            dma((4,)),
        ],
        compiler_params=pltpu.CompilerParams(vmem_limit_bytes=56 * 1024 * 1024),
    )(moved)


def solution(mesh):
    placed = (
        P(None, ("ch", "ctx"), None),
        P(None, "ch", None),
        P("ch", None),
        P("ch", None),
        P("ch"),
        P("ch"),
    )

    def whole(streams, *others):
        return jax.shard_map(
            functools.partial(shards, streams.shape[1]),
            mesh=mesh,
            in_specs=placed,
            out_specs=P("ch", "ctx"),
            check_vma=False,
        )(streams, *others)

    return whole
```

```python
import functools

import jax
import jax.numpy as jnp
from jax import lax
from jax.experimental import pallas as pl
from jax.experimental.pallas import tpu as pltpu
from jax.sharding import PartitionSpec as P

BLOCK = 128
MESH = pl.DeviceIdType.MESH


def split(value):
    high = value.astype(jnp.bfloat16)
    low = (value - high.astype(jnp.float32)).astype(jnp.bfloat16)
    return high, low


def halves(array):
    return array[:, :BLOCK] + array[:, BLOCK:]


def rolled(row):
    tile = pltpu.roll(jnp.broadcast_to(row, (8, BLOCK)), 0, 1, stride=1, stride_axis=0)
    return jnp.concatenate(
        [tile] + [pltpu.roll(tile, turn, 1) for turn in range(8, BLOCK, 8)], axis=0
    )


def picked(array, lane):
    lanes = lax.broadcasted_iota(jnp.int32, array.shape, 1)
    return jnp.sum(jnp.where(lanes == lane, array, 0.0), axis=1, keepdims=True)


def upright(row, offset, width):
    shape = (width, row.shape[1])
    lane = lax.broadcasted_iota(jnp.int32, shape, 1)
    at = lax.broadcasted_iota(jnp.int32, shape, 0) + offset
    return jnp.sum(jnp.where(lane == at, row, 0.0), axis=1, keepdims=True)


def flat(column):
    shape = (column.shape[0], BLOCK)
    diagonal = lax.broadcasted_iota(jnp.int32, shape, 0) == lax.broadcasted_iota(
        jnp.int32, shape, 1
    )
    return jnp.sum(jnp.where(diagonal, column, 0.0), axis=0, keepdims=True)


def causal_mask():
    shape = (BLOCK, BLOCK)
    row = lax.broadcasted_iota(jnp.int32, shape, 0)
    lane = lax.broadcasted_iota(jnp.int32, shape, 1)
    return jnp.where(lane >= row, 1.0, 0.0).astype(jnp.bfloat16)


def short_weights(taps_column, causal):
    high, low = split(rolled(flat(taps_column)))
    now = jnp.concatenate([high * causal, low * causal], axis=1)
    before = jnp.concatenate([high, low], axis=1) - now
    return jnp.concatenate([before, now], axis=0)


def short_filtered(window, m, rows, chosen, weights):
    def block_at(n):
        return window[m, rows, n * BLOCK : (n + 1) * BLOCK]

    now = jnp.concatenate([block_at(n) for n in chosen], axis=0)
    before = jnp.concatenate(
        [block_at(n - 1) if n else jnp.zeros_like(block_at(0)) for n in chosen], axis=0
    )
    both = jnp.concatenate([before, now], axis=1)
    return halves(jnp.dot(both, weights, preferred_element_type=jnp.float32))


def settle(source, target, held, fetched, kept):
    count = kept.shape[0]
    chunks = source.shape[0]
    height = source.shape[1] // count

    def fetch(i, chunk):
        rows = pl.ds(i * height, height)
        lanes = pl.ds(chunk * BLOCK, BLOCK)
        return pltpu.make_async_copy(
            source.at[chunk, rows, :], held.at[rows, lanes], fetched.at[i, chunk]
        )

    def keep(i):
        rows = pl.ds(i * height, height)
        return pltpu.make_async_copy(held.at[rows, :], target.at[rows, :], kept.at[i])

    for i in range(count):
        for chunk in range(chunks):
            fetch(i, chunk).start()
    for i in range(count):
        for chunk in range(chunks):
            fetch(i, chunk).wait()
        keep(i).start()
    for i in range(count):
        keep(i).wait()


def fused(
    total_channels,
    at_once,
    early_steps,
    streams,
    taps,
    pole_rates,
    residues_of,
    skips,
    gains,
    out,
    window,
    gated_at,
    filters,
    tables,
    held_at,
    squares,
    sums,
    scales,
    staged,
    early,
    early_staged,
    fetched,
    early_sent,
    early_got,
    early_kept,
    sums_sent,
    sums_got,
    block_sent,
    block_got,
    kept,
):
    chunks, owners, channels, _ = gated_at.shape
    width = pole_rates.shape[0]
    groups = channels // width
    steps = groups // at_once
    blocks = window.shape[2] // BLOCK
    across_count = lax.axis_size("ch")
    me = lax.axis_index("ctx")
    my_ch = lax.axis_index("ch")
    first_group = me * groups

    def fetch(step):
        rows = pl.ds(pl.multiple_of(step * (at_once * width), 16), at_once * width)
        return pltpu.make_async_copy(
            streams.at[:, rows, :], window.at[:, rows, :], fetched.at[step]
        )

    @pl.loop(0, steps)
    def _(step):
        fetch(step).start()

    def peer_ctx(by):
        return {"ctx": lax.rem(me + by, owners)}

    def peer(by):
        return {
            "ctx": lax.rem(me + lax.div(by, across_count), owners),
            "ch": lax.rem(my_ch + lax.rem(by, across_count), across_count),
        }

    devices = owners * across_count
    barrier = pltpu.get_barrier_semaphore()

    @pl.loop(1, devices)
    def _(by):
        pl.semaphore_signal(barrier, inc=1, device_id=peer(by), device_id_type=MESH)

    causal = causal_mask()

    def rows_of(group):
        return pl.ds(pl.multiple_of(group * width, 16), width)

    def per_channel(values, group):
        at = (first_group + group) * width
        return upright(values[pl.ds(lax.div(at, BLOCK), 1), :], lax.rem(at, BLOCK), width)

    def finish(group, chunk, held):
        chosen = range(chunk, blocks, chunks)
        value = short_filtered(window, 0, rows_of(group), chosen, filters[group])
        high, low, starts = (held[:, i * BLOCK : (i + 1) * BLOCK] for i in range(3))
        convolved = jnp.dot(
            jnp.concatenate([high, low, high, starts], axis=1),
            tables[group],
            preferred_element_type=jnp.float32,
        )
        skip = per_channel(skips, group)
        gain = per_channel(gains, group)
        shaped = (owners, width, BLOCK)
        product = (high.astype(jnp.float32) + low.astype(jnp.float32)).reshape(shaped)
        gated = value.reshape(shaped) * (convolved.reshape(shaped) + skip[None] * product)
        gated_at[chunk, :, rows_of(group), :] = gated * gain[None]
        return jnp.sum((gated * gated).reshape(owners, width // 8, 8, BLOCK), axis=1)

    def begin(group):
        at = first_group + group
        filters[group] = short_weights(picked(taps[0], at), causal)
        product = 1.0
        for m in (1, 2):
            product *= short_filtered(
                window, m, rows_of(group), range(blocks), short_weights(picked(taps[m], at), causal)
            )
        high, low = split(product)
        pair = jnp.concatenate([high, low], axis=1)

        rates = picked(pole_rates[...], at)
        residues = picked(residues_of[...], at)
        lags = lax.broadcasted_iota(jnp.int32, (width, BLOCK), 1).astype(jnp.float32)
        modes = residues * jnp.exp(-rates * lags)
        table_high, table_low = split(rolled(jnp.sum(modes, axis=0, keepdims=True)))
        table_high = table_high * causal
        lift_high, lift_low = split(residues * jnp.exp(-rates * (lags + 1.0)))
        spare = BLOCK - 3 * width
        tables[group] = jnp.concatenate(
            [
                table_high,
                table_high,
                table_low * causal,
                lift_high,
                lift_high,
                lift_low,
                jnp.zeros((spare, BLOCK), jnp.bfloat16),
            ],
            axis=0,
        )

        back_high, back_low = split(jnp.exp(-rates * (BLOCK - 1 - lags)))
        back = jnp.concatenate(
            [
                jnp.concatenate([back_high, back_high], axis=1),
                jnp.concatenate([back_low, back_low], axis=1),
            ],
            axis=0,
        )
        ends = lax.dot_general(
            back, pair, (((1,), (1,)), ((), ())), preferred_element_type=jnp.float32
        )
        states = ends[:width] + ends[width:]
        lane = lax.broadcasted_iota(jnp.int32, states.shape, 1)
        reach = 1
        while reach < blocks:
            earlier = pltpu.roll(states, reach * width, 1)
            decay = jnp.exp(-rates * (BLOCK * reach))
            states = states + jnp.where(lane >= reach * width, decay * earlier, 0.0)
            reach *= 2
        starts = jnp.where(lane >= width, pltpu.roll(states, width, 1), 0.0)
        starts_high, starts_low = (part.astype(jnp.float32) for part in split(starts))
        starts = jnp.concatenate(
            [
                starts_high,
                starts_low,
                starts_high,
                jnp.zeros((spare, starts.shape[1]), jnp.float32),
            ],
            axis=0,
        ).T.astype(jnp.bfloat16)
        held = jnp.concatenate([pair, starts], axis=1)

        def of_chunk(chunk):
            return jnp.concatenate(
                [held[n * width : (n + 1) * width] for n in range(chunk, blocks, chunks)], axis=0
            )

        for chunk in range(1, chunks):
            held_at[chunk - 1, group] = of_chunk(chunk)
        return of_chunk(0)

    early_channels = early_steps * at_once * width

    def early_copy(step, by):
        rows = pl.ds(pl.multiple_of(step * (at_once * width), 16), at_once * width)
        return pltpu.make_async_remote_copy(
            src_ref=gated_at.at[0, lax.rem(me + by, owners), rows, :],
            dst_ref=early.at[by, rows, :],
            send_sem=early_sent.at[step, by],
            recv_sem=early_got.at[step, by],
            device_id=peer_ctx(by),
            device_id_type=MESH,
        )

    def early_keep(by):
        source = lax.rem(me + owners - by, owners)
        return pltpu.make_async_copy(
            early_staged.at[by],
            out.at[0, pl.ds(pl.multiple_of(source * channels, 16), early_channels), :],
            early_kept.at[by],
        )

    def keep_early():
        @pl.loop(1, owners)
        def _(by):
            for step in range(early_steps):
                early_copy(step, by).wait()
            row = scales[0, pl.ds(me, 1), :]
            early_staged[by] = (early[by] * row).astype(jnp.bfloat16)
            early_keep(by).start()

    squares[...] = jnp.zeros_like(squares)

    @pl.loop(0, steps)
    def _(step):
        fetch(step).wait()
        begun = [begin(step * at_once + i) for i in range(at_once)]
        for i, held in enumerate(begun):
            squares[0] += finish(step * at_once + i, 0, held)

        if early_steps:

            @pl.when(step == 0)
            def _():
                pl.semaphore_wait(barrier, devices - 1)

            @pl.when(step < early_steps)
            def _():
                @pl.loop(1, owners)
                def _(by):
                    early_copy(step, by).start()

    def later(chunk, low, high):
        @pl.loop(low, high)
        def _(step):
            total = 0.0
            for i in range(at_once):
                group = step * at_once + i
                total += finish(group, chunk, held_at[chunk - 1, group])
            squares[chunk] += total

    def sums_copy(chunk, by):
        return pltpu.make_async_remote_copy(
            src_ref=sums.at[chunk, 0],
            dst_ref=sums.at[chunk, by],
            send_sem=sums_sent.at[chunk, by],
            recv_sem=sums_got.at[chunk, by],
            device_id=peer(by),
            device_id_type=MESH,
        )

    def place(chunk, owner, first):
        return out.at[
            chunk, pl.ds(pl.multiple_of(owner * channels + first, 16), channels - first), :
        ]

    def first_of(chunk):
        return early_channels if chunk == 0 else 0

    def block_copy(chunk, by, owner):
        first = first_of(chunk)
        return pltpu.make_async_remote_copy(
            src_ref=staged.at[chunk, by, first:, :],
            dst_ref=place(chunk, owner, first),
            send_sem=block_sent.at[chunk, by],
            recv_sem=block_got.at[chunk, by],
            device_id=peer_ctx(by),
            device_id_type=MESH,
        )

    def own_copy(chunk):
        return pltpu.make_async_copy(
            staged.at[chunk, 0], place(chunk, me, 0), kept.at[chunk]
        )

    def start_sums(chunk):
        sums[chunk, 0] = jnp.sum(squares[chunk], axis=1)

        @pl.loop(1, devices)
        def _(by):
            sums_copy(chunk, by).start()

    def start_blocks(chunk):
        @pl.loop(1, devices)
        def _(by):
            sums_copy(chunk, by).wait()

        total = jnp.sum(sums[chunk], axis=0)
        scales[chunk] = lax.rsqrt(total / total_channels + 1e-05)

        def fill(by, first):
            target = lax.rem(me + by, owners)
            row = scales[chunk, pl.ds(target, 1), :]
            staged[chunk, by, first:, :] = (gated_at[chunk, target, first:, :] * row).astype(
                jnp.bfloat16
            )

        @pl.loop(1, owners)
        def _(by):
            fill(by, first_of(chunk))
            block_copy(chunk, by, me).start()

        fill(0, 0)
        own_copy(chunk).start()

    def wait_blocks(chunk):
        own_copy(chunk).wait()

        @pl.loop(1, owners)
        def _(by):
            block_copy(chunk, by, me).wait_send()
            block_copy(chunk, by, lax.rem(me + owners - by, owners)).wait_recv()

    if not early_steps:
        pl.semaphore_wait(barrier, devices - 1)
    start_sums(0)
    for chunk in range(chunks):
        if chunk + 1 < chunks:
            later(chunk + 1, 0, steps)
            start_sums(chunk + 1)
        start_blocks(chunk)
    if early_steps:
        keep_early()
    for chunk in range(chunks):
        wait_blocks(chunk)
    if early_steps:

        @pl.loop(1, owners)
        def _(by):
            early_keep(by).wait()


def shards(total_channels, streams, short_taps, pole_rates, residues, skip, gain):
    owners = lax.axis_size("ctx")
    across = lax.axis_size("ch")
    channels, length = streams.shape[1:]
    groups = pole_rates.shape[0] // owners
    width = channels // groups
    assert pole_rates.shape[1] == width
    own = length // owners
    chunks = own // BLOCK
    later = max(chunks - 1, 1)
    devices = owners * across
    at_once = next(n for n in (2, 1) if groups % n == 0)
    steps = groups // at_once
    early_steps = 3 * steps // 4
    early_channels = max(early_steps, 1) * at_once * width
    vmem = pltpu.VMEM
    dma = pltpu.SemaphoreType.DMA
    f32 = jnp.float32
    bf16 = jnp.bfloat16
    moved = pl.pallas_call(
        functools.partial(fused, total_channels, at_once, early_steps),
        in_specs=[pl.BlockSpec(memory_space=pltpu.HBM)] + [pl.BlockSpec(memory_space=vmem)] * 5,
        out_specs=pl.BlockSpec(memory_space=pl.ANY),
        out_shape=jax.ShapeDtypeStruct((chunks, owners * channels, BLOCK), bf16),
        scratch_shapes=[
            vmem(streams.shape, bf16),
            vmem((chunks, owners, channels, BLOCK), f32),
            vmem((groups, 2 * BLOCK, 2 * BLOCK), bf16),
            vmem((groups, 4 * BLOCK, BLOCK), bf16),
            vmem((later, groups, owners * width, 3 * BLOCK), bf16),
            vmem((chunks, owners, 8, BLOCK), f32),
            vmem((chunks, devices, owners, BLOCK), f32),
            vmem((chunks, owners, BLOCK), f32),
            vmem((chunks, owners, channels, BLOCK), bf16),
            vmem((owners, early_channels, BLOCK), f32),
            vmem((owners, early_channels, BLOCK), bf16),
            dma((steps,)),
            dma((max(early_steps, 1), owners)),
            dma((max(early_steps, 1), owners)),
            dma((owners,)),
            dma((chunks, devices)),
            dma((chunks, devices)),
            dma((chunks, owners)),
            dma((chunks, owners)),
            dma((chunks,)),
        ],
        compiler_params=pltpu.CompilerParams(
            collective_id=0, has_side_effects=True, vmem_limit_bytes=56 * 1024 * 1024
        ),
    )(
        streams,
        short_taps.transpose(0, 2, 1),
        pole_rates.T,
        residues.T,
        skip.reshape(-1, BLOCK),
        gain.reshape(-1, BLOCK),
    )
    return pl.pallas_call(
        settle,
        in_specs=[pl.BlockSpec(memory_space=pl.ANY)],
        out_specs=pl.BlockSpec(memory_space=pl.ANY),
        out_shape=jax.ShapeDtypeStruct((owners * channels, own), bf16),
        scratch_shapes=[
            vmem((owners * channels, own), bf16),
            dma((4, chunks)),
            dma((4,)),
        ],
        compiler_params=pltpu.CompilerParams(vmem_limit_bytes=56 * 1024 * 1024),
    )(moved)


def solution(mesh):
    placed = (
        P(None, ("ch", "ctx"), None),
        P(None, "ch", None),
        P("ch", None),
        P("ch", None),
        P("ch"),
        P("ch"),
    )

    def whole(streams, *others):
        return jax.shard_map(
            functools.partial(shards, streams.shape[1]),
            mesh=mesh,
            in_specs=placed,
            out_specs=P("ch", "ctx"),
            check_vma=False,
        )(streams, *others)

    return whole
```

```python
import functools

import jax
import jax.numpy as jnp
from jax import lax
from jax.experimental import pallas as pl
from jax.experimental.pallas import tpu as pltpu
from jax.sharding import PartitionSpec as P

BLOCK = 128
MESH = pl.DeviceIdType.MESH


def split(value):
    high = value.astype(jnp.bfloat16)
    low = (value - high.astype(jnp.float32)).astype(jnp.bfloat16)
    return high, low


def halves(array):
    return array[:, :BLOCK] + array[:, BLOCK:]


def rolled(row):
    tile = pltpu.roll(jnp.broadcast_to(row, (8, BLOCK)), 0, 1, stride=1, stride_axis=0)
    return jnp.concatenate(
        [tile] + [pltpu.roll(tile, turn, 1) for turn in range(8, BLOCK, 8)], axis=0
    )


def picked(array, lane):
    lanes = lax.broadcasted_iota(jnp.int32, array.shape, 1)
    return jnp.sum(jnp.where(lanes == lane, array, 0.0), axis=1, keepdims=True)


def upright(row, offset, width):
    shape = (width, row.shape[1])
    lane = lax.broadcasted_iota(jnp.int32, shape, 1)
    at = lax.broadcasted_iota(jnp.int32, shape, 0) + offset
    return jnp.sum(jnp.where(lane == at, row, 0.0), axis=1, keepdims=True)


def flat(column):
    shape = (column.shape[0], BLOCK)
    diagonal = lax.broadcasted_iota(jnp.int32, shape, 0) == lax.broadcasted_iota(
        jnp.int32, shape, 1
    )
    return jnp.sum(jnp.where(diagonal, column, 0.0), axis=0, keepdims=True)


def causal_mask():
    shape = (BLOCK, BLOCK)
    row = lax.broadcasted_iota(jnp.int32, shape, 0)
    lane = lax.broadcasted_iota(jnp.int32, shape, 1)
    return jnp.where(lane >= row, 1.0, 0.0).astype(jnp.bfloat16)


def short_weights(taps_column, causal):
    high, low = split(rolled(flat(taps_column)))
    now = jnp.concatenate([high * causal, low * causal], axis=1)
    before = jnp.concatenate([high, low], axis=1) - now
    return jnp.concatenate([before, now], axis=0)


def short_filtered(window, m, rows, chosen, weights):
    def block_at(n):
        return window[m, rows, n * BLOCK : (n + 1) * BLOCK]

    now = jnp.concatenate([block_at(n) for n in chosen], axis=0)
    before = jnp.concatenate(
        [block_at(n - 1) if n else jnp.zeros_like(block_at(0)) for n in chosen], axis=0
    )
    both = jnp.concatenate([before, now], axis=1)
    return halves(jnp.dot(both, weights, preferred_element_type=jnp.float32))


def settle(source, target, held, fetched, kept):
    count = kept.shape[0]
    chunks = source.shape[0]
    height = source.shape[1] // count

    def fetch(i, chunk):
        rows = pl.ds(i * height, height)
        lanes = pl.ds(chunk * BLOCK, BLOCK)
        return pltpu.make_async_copy(
            source.at[chunk, rows, :], held.at[rows, lanes], fetched.at[i, chunk]
        )

    def keep(i):
        rows = pl.ds(i * height, height)
        return pltpu.make_async_copy(held.at[rows, :], target.at[rows, :], kept.at[i])

    for i in range(count):
        for chunk in range(chunks):
            fetch(i, chunk).start()
    for i in range(count):
        for chunk in range(chunks):
            fetch(i, chunk).wait()
        keep(i).start()
    for i in range(count):
        keep(i).wait()


def fused(
    total_channels,
    at_once,
    early_steps,
    streams,
    taps,
    pole_rates,
    residues_of,
    skips,
    gains,
    out,
    window,
    gated_at,
    filters,
    tables,
    held_at,
    squares,
    sums,
    scales,
    staged,
    early,
    early_staged,
    fetched,
    early_sent,
    early_got,
    early_kept,
    sums_sent,
    sums_got,
    block_sent,
    block_got,
    kept,
):
    chunks, owners, channels, _ = gated_at.shape
    width = pole_rates.shape[0]
    groups = channels // width
    steps = groups // at_once
    blocks = window.shape[2] // BLOCK
    across_count = lax.axis_size("ch")
    me = lax.axis_index("ctx")
    my_ch = lax.axis_index("ch")
    first_group = me * groups

    def fetch(step):
        rows = pl.ds(pl.multiple_of(step * (at_once * width), 16), at_once * width)
        return pltpu.make_async_copy(
            streams.at[:, rows, :], window.at[:, rows, :], fetched.at[step]
        )

    @pl.loop(0, steps)
    def _(step):
        fetch(step).start()

    def peer_ctx(by):
        return {"ctx": lax.rem(me + by, owners)}

    def peer(by):
        return {
            "ctx": lax.rem(me + lax.div(by, across_count), owners),
            "ch": lax.rem(my_ch + lax.rem(by, across_count), across_count),
        }

    devices = owners * across_count
    barrier = pltpu.get_barrier_semaphore()

    @pl.loop(1, devices)
    def _(by):
        pl.semaphore_signal(barrier, inc=1, device_id=peer(by), device_id_type=MESH)

    causal = causal_mask()

    def rows_of(group):
        return pl.ds(pl.multiple_of(group * width, 16), width)

    def per_channel(values, group):
        at = (first_group + group) * width
        return upright(values[pl.ds(lax.div(at, BLOCK), 1), :], lax.rem(at, BLOCK), width)

    def finish(group, chunk, held):
        chosen = range(chunk, blocks, chunks)
        value = short_filtered(window, 0, rows_of(group), chosen, filters[group])
        high, low, starts = (held[:, i * BLOCK : (i + 1) * BLOCK] for i in range(3))
        convolved = jnp.dot(
            jnp.concatenate([high, low, high, starts], axis=1),
            tables[group],
            preferred_element_type=jnp.float32,
        )
        skip = per_channel(skips, group)
        gain = per_channel(gains, group)
        shaped = (owners, width, BLOCK)
        product = (high.astype(jnp.float32) + low.astype(jnp.float32)).reshape(shaped)
        gated = value.reshape(shaped) * (convolved.reshape(shaped) + skip[None] * product)
        gated_at[chunk, :, rows_of(group), :] = gated * gain[None]
        return jnp.sum((gated * gated).reshape(owners, width // 8, 8, BLOCK), axis=1)

    def begin(group):
        at = first_group + group
        filters[group] = short_weights(picked(taps[0], at), causal)
        product = 1.0
        for m in (1, 2):
            product *= short_filtered(
                window, m, rows_of(group), range(blocks), short_weights(picked(taps[m], at), causal)
            )
        high, low = split(product)
        pair = jnp.concatenate([high, low], axis=1)

        rates = picked(pole_rates[...], at)
        residues = picked(residues_of[...], at)
        lags = lax.broadcasted_iota(jnp.int32, (width, BLOCK), 1).astype(jnp.float32)
        modes = residues * jnp.exp(-rates * lags)
        table_high, table_low = split(rolled(jnp.sum(modes, axis=0, keepdims=True)))
        table_high = table_high * causal
        lift_high, lift_low = split(residues * jnp.exp(-rates * (lags + 1.0)))
        spare = BLOCK - 3 * width
        tables[group] = jnp.concatenate(
            [
                table_high,
                table_high,
                table_low * causal,
                lift_high,
                lift_high,
                lift_low,
                jnp.zeros((spare, BLOCK), jnp.bfloat16),
            ],
            axis=0,
        )

        back_high, back_low = split(jnp.exp(-rates * (BLOCK - 1 - lags)))
        back = jnp.concatenate(
            [
                jnp.concatenate([back_high, back_high], axis=1),
                jnp.concatenate([back_low, back_low], axis=1),
            ],
            axis=0,
        )
        ends = lax.dot_general(
            back, pair, (((1,), (1,)), ((), ())), preferred_element_type=jnp.float32
        )
        states = ends[:width] + ends[width:]
        lane = lax.broadcasted_iota(jnp.int32, states.shape, 1)
        reach = 1
        while reach < blocks:
            earlier = pltpu.roll(states, reach * width, 1)
            decay = jnp.exp(-rates * (BLOCK * reach))
            states = states + jnp.where(lane >= reach * width, decay * earlier, 0.0)
            reach *= 2
        starts = jnp.where(lane >= width, pltpu.roll(states, width, 1), 0.0)
        starts_high, starts_low = (part.astype(jnp.float32) for part in split(starts))
        starts = jnp.concatenate(
            [
                starts_high,
                starts_low,
                starts_high,
                jnp.zeros((spare, starts.shape[1]), jnp.float32),
            ],
            axis=0,
        ).T.astype(jnp.bfloat16)
        held = jnp.concatenate([pair, starts], axis=1)

        def of_chunk(chunk):
            return jnp.concatenate(
                [held[n * width : (n + 1) * width] for n in range(chunk, blocks, chunks)], axis=0
            )

        for chunk in range(1, chunks):
            held_at[chunk - 1, group] = of_chunk(chunk)
        return of_chunk(0)

    early_channels = early_steps * at_once * width

    def early_copy(step, by):
        rows = pl.ds(pl.multiple_of(step * (at_once * width), 16), at_once * width)
        return pltpu.make_async_remote_copy(
            src_ref=gated_at.at[0, lax.rem(me + by, owners), rows, :],
            dst_ref=early.at[by, rows, :],
            send_sem=early_sent.at[step, by],
            recv_sem=early_got.at[step, by],
            device_id=peer_ctx(by),
            device_id_type=MESH,
        )

    def early_keep(by):
        source = lax.rem(me + owners - by, owners)
        return pltpu.make_async_copy(
            early_staged.at[by],
            out.at[0, pl.ds(pl.multiple_of(source * channels, 16), early_channels), :],
            early_kept.at[by],
        )

    def keep_early():
        @pl.loop(1, owners)
        def _(by):
            for step in range(early_steps):
                early_copy(step, by).wait()
            row = scales[0, pl.ds(me, 1), :]
            early_staged[by] = (early[by] * row).astype(jnp.bfloat16)
            early_keep(by).start()

    squares[...] = jnp.zeros_like(squares)

    @pl.loop(0, steps)
    def _(step):
        fetch(step).wait()
        begun = [begin(step * at_once + i) for i in range(at_once)]
        for i, held in enumerate(begun):
            squares[0] += finish(step * at_once + i, 0, held)

        if early_steps:

            @pl.when(step == 0)
            def _():
                pl.semaphore_wait(barrier, devices - 1)

            @pl.when(step < early_steps)
            def _():
                @pl.loop(1, owners)
                def _(by):
                    early_copy(step, by).start()

    def later(chunk, low, high):
        @pl.loop(low, high)
        def _(step):
            total = 0.0
            for i in range(at_once):
                group = step * at_once + i
                total += finish(group, chunk, held_at[chunk - 1, group])
            squares[chunk] += total

    def sums_copy(chunk, by):
        return pltpu.make_async_remote_copy(
            src_ref=sums.at[chunk, 0],
            dst_ref=sums.at[chunk, by],
            send_sem=sums_sent.at[chunk, by],
            recv_sem=sums_got.at[chunk, by],
            device_id=peer(by),
            device_id_type=MESH,
        )

    def place(chunk, owner, first):
        return out.at[
            chunk, pl.ds(pl.multiple_of(owner * channels + first, 16), channels - first), :
        ]

    def first_of(chunk):
        return early_channels if chunk == 0 else 0

    def block_copy(chunk, by, owner):
        first = first_of(chunk)
        return pltpu.make_async_remote_copy(
            src_ref=staged.at[chunk, by, first:, :],
            dst_ref=place(chunk, owner, first),
            send_sem=block_sent.at[chunk, by],
            recv_sem=block_got.at[chunk, by],
            device_id=peer_ctx(by),
            device_id_type=MESH,
        )

    def own_copy(chunk):
        return pltpu.make_async_copy(
            staged.at[chunk, 0], place(chunk, me, 0), kept.at[chunk]
        )

    def start_sums(chunk):
        sums[chunk, 0] = jnp.sum(squares[chunk], axis=1)

        @pl.loop(1, devices)
        def _(by):
            sums_copy(chunk, by).start()

    def start_blocks(chunk):
        @pl.loop(1, devices)
        def _(by):
            sums_copy(chunk, by).wait()

        total = jnp.sum(sums[chunk], axis=0)
        scales[chunk] = lax.rsqrt(total / total_channels + 1e-05)

        def fill(by, first):
            target = lax.rem(me + by, owners)
            row = scales[chunk, pl.ds(target, 1), :]
            staged[chunk, by, first:, :] = (gated_at[chunk, target, first:, :] * row).astype(
                jnp.bfloat16
            )

        @pl.loop(1, owners)
        def _(by):
            fill(by, first_of(chunk))
            block_copy(chunk, by, me).start()

        fill(0, 0)
        own_copy(chunk).start()

    def wait_blocks(chunk):
        own_copy(chunk).wait()

        @pl.loop(1, owners)
        def _(by):
            block_copy(chunk, by, me).wait_send()
            block_copy(chunk, by, lax.rem(me + owners - by, owners)).wait_recv()

    if not early_steps:
        pl.semaphore_wait(barrier, devices - 1)
    start_sums(0)
    for chunk in range(chunks):
        if chunk + 1 < chunks:
            later(chunk + 1, 0, steps)
            start_sums(chunk + 1)
        start_blocks(chunk)
    if early_steps:
        keep_early()
    for chunk in range(chunks):
        wait_blocks(chunk)
    if early_steps:

        @pl.loop(1, owners)
        def _(by):
            early_keep(by).wait()


def shards(total_channels, streams, short_taps, pole_rates, residues, skip, gain):
    owners = lax.axis_size("ctx")
    across = lax.axis_size("ch")
    channels, length = streams.shape[1:]
    groups = pole_rates.shape[0] // owners
    width = channels // groups
    assert pole_rates.shape[1] == width
    own = length // owners
    chunks = own // BLOCK
    later = max(chunks - 1, 1)
    devices = owners * across
    at_once = next(n for n in (2, 1) if groups % n == 0)
    steps = groups // at_once
    early_steps = 3 * steps // 8
    early_channels = max(early_steps, 1) * at_once * width
    vmem = pltpu.VMEM
    dma = pltpu.SemaphoreType.DMA
    f32 = jnp.float32
    bf16 = jnp.bfloat16
    moved = pl.pallas_call(
        functools.partial(fused, total_channels, at_once, early_steps),
        in_specs=[pl.BlockSpec(memory_space=pltpu.HBM)] + [pl.BlockSpec(memory_space=vmem)] * 5,
        out_specs=pl.BlockSpec(memory_space=pl.ANY),
        out_shape=jax.ShapeDtypeStruct((chunks, owners * channels, BLOCK), bf16),
        scratch_shapes=[
            vmem(streams.shape, bf16),
            vmem((chunks, owners, channels, BLOCK), f32),
            vmem((groups, 2 * BLOCK, 2 * BLOCK), bf16),
            vmem((groups, 4 * BLOCK, BLOCK), bf16),
            vmem((later, groups, owners * width, 3 * BLOCK), bf16),
            vmem((chunks, owners, 8, BLOCK), f32),
            vmem((chunks, devices, owners, BLOCK), f32),
            vmem((chunks, owners, BLOCK), f32),
            vmem((chunks, owners, channels, BLOCK), bf16),
            vmem((owners, early_channels, BLOCK), f32),
            vmem((owners, early_channels, BLOCK), bf16),
            dma((steps,)),
            dma((max(early_steps, 1), owners)),
            dma((max(early_steps, 1), owners)),
            dma((owners,)),
            dma((chunks, devices)),
            dma((chunks, devices)),
            dma((chunks, owners)),
            dma((chunks, owners)),
            dma((chunks,)),
        ],
        compiler_params=pltpu.CompilerParams(
            collective_id=0, has_side_effects=True, vmem_limit_bytes=56 * 1024 * 1024
        ),
    )(
        streams,
        short_taps.transpose(0, 2, 1),
        pole_rates.T,
        residues.T,
        skip.reshape(-1, BLOCK),
        gain.reshape(-1, BLOCK),
    )
    return pl.pallas_call(
        settle,
        in_specs=[pl.BlockSpec(memory_space=pl.ANY)],
        out_specs=pl.BlockSpec(memory_space=pl.ANY),
        out_shape=jax.ShapeDtypeStruct((owners * channels, own), bf16),
        scratch_shapes=[
            vmem((owners * channels, own), bf16),
            dma((4, chunks)),
            dma((4,)),
        ],
        compiler_params=pltpu.CompilerParams(vmem_limit_bytes=56 * 1024 * 1024),
    )(moved)


def solution(mesh):
    placed = (
        P(None, ("ch", "ctx"), None),
        P(None, "ch", None),
        P("ch", None),
        P("ch", None),
        P("ch"),
        P("ch"),
    )

    def whole(streams, *others):
        return jax.shard_map(
            functools.partial(shards, streams.shape[1]),
            mesh=mesh,
            in_specs=placed,
            out_specs=P("ch", "ctx"),
            check_vma=False,
        )(streams, *others)

    return whole
```
